128 devices in a mesh: tm: 16 (over x, y), sy: 4 (over z), sx: 2 (over core).
Axes of the slice: x: 4, y: 4, z: 4, core: 2. Of those that a mesh axis runs over, the one named last changes fastest.
Arguments:
- latent: bfloat16 [32, 128, 64, 16], P('tm', 'sy', 'sx'), may hold values from -6 to 6
- clip_lengths: int32 [9], replicated, may hold values from 1 to 16, as said below
- entry_kernel: bfloat16 [3, 3, 3, 16, 384], replicated, may hold values from -0.3125 to 0.3125
- first_gain: float32 [384], replicated, may hold values from 0.25 to 1.75
- first_kernel: bfloat16 [3, 3, 3, 384, 384], replicated, may hold values from -0.0625 to 0.0625
- second_gain: float32 [384], replicated, may hold values from 0.25 to 1.75
- second_kernel: bfloat16 [3, 3, 3, 384, 384], replicated, may hold values from -0.0625 to 0.0625
Outputs:
- decoded: bfloat16 [32, 128, 64, 384], P('tm', 'sy', 'sx')
The draws below stay inside these ranges and needn't reach their ends.
Inputs may be any that keep to these rules, and one draw needn't show every extreme that they name: `clip_lengths`: 9 clips packed in order; their lengths sum to 32; the last clip is the longest, with exactly 16 frames.
All inputs are finite; a program needn't handle non-finite values.
Results may differ from the reference program's by a relative error of at most 0.015.
Values may be sent and summed in bfloat16 or wider, within the bound.
A program may use at most 192 MiB of HBM per device.

```python
import jax
import jax.numpy as jnp
from jax import lax

Z = 16
C = 384
TOTAL_F = 32
H = 128
W = 64
CLIPS = 9
MOST_LEN = 16


def draw_clip_lengths(key, part):
    key = jax.random.fold_in(key, 7)
    remainder = TOTAL_F - MOST_LEN
    order = jax.random.permutation(key, remainder - 1).astype(jnp.int32) + 1
    cuts = jnp.sort(order[:CLIPS - 2]).astype(jnp.int32)
    bounds = jnp.concatenate([jnp.zeros((1,), jnp.int32), cuts, jnp.full((1,), remainder, jnp.int32)])
    others = (bounds[1:] - bounds[:-1]).astype(jnp.int32)
    return jnp.concatenate([others, jnp.full((1,), MOST_LEN, jnp.int32)]).astype(jnp.int32)


def steps_of(key, dims, split, least, largest):
    def one(dim, blocks):
        steps = jax.random.uniform(jax.random.fold_in(jax.random.fold_in(key, 6), dim), (blocks,), jnp.float32, least / len(split), largest / len(split))
        return jnp.repeat(jnp.exp(steps), dims[dim] // blocks).reshape((-1,) + (1,) * (len(dims) - dim - 1))

    gain = one(*split[0])
    for cut in split[1:]:
        gain = gain * one(*cut)
    return gain


def gaussian(rng, dims, spread, bound, split=(), kind=jnp.bfloat16):
    loudness = steps_of(rng, dims, split, -0.22, 0.18) if split else 1.0
    entries = jax.random.normal(rng, dims, jnp.float32) * spread * loudness
    return jnp.minimum(jnp.maximum(entries, -bound), bound).astype(kind)


def setup_inputs(seed: int = 0) -> dict:
    streams_of = jax.random.split(jax.random.key(seed), 8)
    return {
        "latent": gaussian(streams_of[0], (TOTAL_F, H, W, Z), 1.0, 6.0, ((0, 16), (1, 4), (2, 2))),
        "clip_lengths": draw_clip_lengths(jax.random.fold_in(streams_of[7], 71), 0),
        "entry_kernel": gaussian(streams_of[2], (3, 3, 3, Z, C), (27 * Z) ** -0.5, 0.3125),
        "first_gain": jnp.clip(1.0 + 0.15 * jax.random.normal(streams_of[3], (C,), jnp.float32), 0.25, 1.75),
        "first_kernel": gaussian(streams_of[4], (3, 3, 3, C, C), (27 * C) ** -0.5, 0.0625),
        "second_gain": jnp.clip(1.0 + 0.15 * jax.random.normal(streams_of[5], (C,), jnp.float32), 0.25, 1.75),
        "second_kernel": gaussian(streams_of[6], (3, 3, 3, C, C), (27 * C) ** -0.5, 0.0625),
    }


def clip_distance(clip_lengths, positions):
    lengths = clip_lengths.astype(jnp.int32)
    starts = (jnp.cumsum(lengths) - lengths).astype(jnp.int32)
    earlier = starts[None, :] <= positions[:, None]
    latest = lax.optimization_barrier(jnp.max(jnp.where(earlier, starts[None, :], -1), axis=1)).astype(jnp.int32)
    return (positions - latest).astype(jnp.int32)

def spatial_conv(frames, kernel):
    return lax.conv_general_dilated(frames, kernel, (1, 1), 'VALID', dimension_numbers=('NHWC', 'HWIO', 'NHWC'), preferred_element_type=jnp.float32)

def causal_conv(padded, kernel, distance):
    count_out = padded.shape[0] - 2
    summed = jnp.zeros((count_out, padded.shape[1] - 2, padded.shape[2] - 2, kernel.shape[-1]), jnp.float32)
    for frame_lag in range(3):
        partial_term = spatial_conv(padded[2 - frame_lag:2 - frame_lag + count_out], kernel[2 - frame_lag])
        keep_mask = (distance >= frame_lag).astype(jnp.float32)
        summed = summed + keep_mask[:, None, None, None] * partial_term
    return summed

def norm_act(values, gain_vec):
    values = values.astype(jnp.float32)
    scaled = values * lax.rsqrt(lax.optimization_barrier(jnp.mean(values * values, axis=-1, keepdims=True)) + 1e-06) * gain_vec
    return jax.nn.silu(scaled).astype(jnp.bfloat16)

def pad_full(values):
    return jnp.pad(values, ((2, 0), (1, 1), (1, 1), (0, 0)))

def reference(latent, clip_lengths, entry_kernel, first_gain, first_kernel, second_gain, second_kernel):
    positions = jnp.arange(latent.shape[0], dtype=jnp.int32)
    distance = clip_distance(clip_lengths, positions)
    entry = causal_conv(pad_full(latent), entry_kernel, distance).astype(jnp.bfloat16)
    first_act = norm_act(entry, first_gain)
    middle = causal_conv(pad_full(first_act), first_kernel, distance)
    second_act = norm_act(middle, second_gain)
    branch = causal_conv(pad_full(second_act), second_kernel, distance)
    return (entry.astype(jnp.float32) + branch).astype(jnp.bfloat16)
```

```python
import functools

import jax
import jax.numpy as jnp
from jax import lax
from jax.experimental import pallas as pl
from jax.experimental.pallas import tpu as pltpu
from jax.sharding import PartitionSpec as P

C = 384
K3 = 3 * C
MIB = 2**20
BF = jnp.bfloat16
F32 = jnp.float32


def passed_along(block, axis, distance):
    devices = range(lax.axis_size(axis))
    route = [(i - distance, i) for i in devices if i - distance in devices]
    return lax.ppermute(block, axis, route)


def padded(block, sides, width):
    for axis, dim in sides:
        count = lax.axis_size(axis)
        forward = [(i, i + 1) for i in range(count - 1)]
        backward = [(target, source) for source, target in forward]
        low = lax.ppermute(
            lax.slice_in_dim(block, block.shape[dim] - width, None, axis=dim), axis, forward
        )
        high = lax.ppermute(lax.slice_in_dim(block, 0, width, axis=dim), axis, backward)
        block = jnp.concatenate([low, block, high], axis=dim)
    return block


def clip_distance(clip_lengths, positions):
    starts = jnp.cumsum(clip_lengths) - clip_lengths
    earlier = starts[None, :] <= positions[:, None]
    latest = jnp.max(jnp.where(earlier, starts[None, :], -1), axis=1)
    return positions - latest


def weights_kernel(w_ref, u_ref):
    step = 16

    @pl.loop(0, w_ref.shape[3] // step)
    def _(block):
        part = pl.ds(pl.multiple_of(block * step, step), step)
        w = [[w_ref[t, y, 0, part, :].astype(F32) for y in range(3)] for t in range(3)]

        def rows(g, out):
            u_ref[out, 0, 0, part, :] = g[0].astype(BF)
            edge = g[0] + g[2]
            u_ref[out, 1, 0, part, :] = ((edge + g[1]) * 0.5).astype(BF)
            u_ref[out, 2, 0, part, :] = ((edge - g[1]) * 0.5).astype(BF)
            u_ref[out, 3, 0, part, :] = g[2].astype(BF)

        rows(w[0], 0)
        rows([(w[0][y] + w[2][y] + w[1][y]) * 0.5 for y in range(3)], 1)
        rows([(w[0][y] + w[2][y] - w[1][y]) * 0.5 for y in range(3)], 2)
        rows(w[2], 3)
        rows(w[1], 4)


def transformed_weights(kernel):
    chunk = 128
    return pl.pallas_call(
        weights_kernel,
        grid=(3, C // chunk),
        in_specs=[pl.BlockSpec((3, 3, 1, chunk, C), lambda x, c: (0, 0, x, c, 0))],
        out_specs=pl.BlockSpec((5, 4, 1, chunk, C), lambda x, c: (0, 0, x, c, 0)),
        out_shape=jax.ShapeDtypeStruct((5, 4, 3, C, C), BF),
        compiler_params=pltpu.CompilerParams(vmem_limit_bytes=32 * MIB),
        cost_estimate=pl.CostEstimate(
            flops=30 * 3 * C * C * 3, bytes_accessed=47 * 3 * C * C * 2, transcendentals=0
        ),
        name="weights",
    )(kernel).reshape(5, 4, K3, C)


ROWS = 32
COLS = 32
WIDE = 40
LEAD = 9
CELLS = 256
R1 = ROWS + 4
R2 = ROWS + 2
I1 = R2 // 2
I2 = ROWS // 2
M1 = I1 * COLS + 32
M2 = I2 * COLS
HALF = 24
ENTRY_ROWS = 4


def norm_act(values, gain, keep):
    mean = jnp.mean(values * values, axis=-1, keepdims=True)
    half = values * (lax.rsqrt(mean + 1e-6) * keep) * gain
    return half * jnp.tanh(half) + half


def splat(value, shape):
    one = jnp.full((16, 128), value, F32).astype(BF)
    return jnp.tile(one, (shape[0] // 16, shape[1] // 128))


def main_kernel(
    ints, coefs, q_ref, we_ref, keep_ref, g1_ref, g2_ref, u1_hbm, u2_hbm,
    out_ref,
    f_ref, h_ref, s_ref, e_ref, x_ref, m_ref, acc_ref, w_ref, a_ref, b_ref, hn_ref, sem,
):
    halo_place = ints[0]
    top = ints[1]
    bottom = ints[2]
    halo_slot = ints[3]
    zero_slot = ints[4]

    def fetch(step, slot, source=u1_hbm):
        which = ints[8 + step]
        return pltpu.make_async_copy(source.at[which], w_ref.at[slot], sem.at[slot])

    fetch(0, 0).start()

    h_ref[...] = jnp.zeros_like(h_ref)

    @pl.loop(0, R1 // ENTRY_ROWS)
    def _(block):
        cols = []
        for n in range(ENTRY_ROWS):
            first = pl.multiple_of((block * ENTRY_ROWS + n) * 16, 16)
            cols.append(
                jnp.concatenate([q_ref[k, pl.ds(first, 48), :] for k in range(9)], axis=0)
            )
        patches = jnp.concatenate(cols, axis=1)
        entry = lax.dot_general(
            patches, we_ref[...], (((0,), (0,)), ((), ())), preferred_element_type=F32
        ).astype(BF)
        for n in range(ENTRY_ROWS):
            row = block * ENTRY_ROWS + n
            inside = jnp.where(row < 2, top, jnp.where(row >= R1 - 2, bottom, 1)).astype(F32)
            value = entry[n * CELLS : (n + 1) * CELLS].astype(F32)
            b_ref[n] = value
            a_ref[n] = norm_act(value, g1_ref[...], keep_ref[...] * inside)
        for n in range(ENTRY_ROWS):
            row = block * ENTRY_ROWS + n
            for f in range(2):
                e_ref[f, row] = b_ref[n, pl.ds((4 + f) * WIDE + LEAD, COLS), :].astype(BF)
            for f in range(6):
                for dx in range(3):
                    lanes = slice(dx * C, (dx + 1) * C)
                    place = f * WIDE + LEAD - 1 + dx
                    f_ref[f, row, :, lanes] = a_ref[n, pl.ds(place, COLS), :].astype(BF)
                    h_ref[f, n % 2, pl.ds(row // 2, 1), lanes] = a_ref[
                        n, pl.ds(f * WIDE + halo_place + dx, 1), :
                    ]

    def products(step, slot, rows):
        for k in range(4):
            m_ref[k, :rows, :] = jnp.dot(
                x_ref[k, :rows, :], w_ref[slot, k], preferred_element_type=F32
            )
        first = coefs[step, 2]
        second = coefs[step, 3]

        @pl.loop(0, rows // COLS)
        def _(i):
            part = pl.ds(pl.multiple_of(i * COLS, COLS), COLS)
            terms = [m_ref[k, part, :] for k in range(4)]
            even = terms[0] + terms[1] + terms[2]
            odd = terms[1] - terms[2] - terms[3]
            for parity, value in enumerate((even, odd)):
                acc_ref[0, parity, part, :] += first * value
                acc_ref[1, parity, part, :] += second * value

    def row_transform(d):
        return d[0] - d[2], d[1] + d[2], d[2] - d[1], d[1] - d[3]

    def frames_of(tau, base):
        one = jnp.where(tau == 0, 0, jnp.where(tau == 2, 2, 1)) + base
        other = jnp.where(tau == 2, 1, jnp.where(tau == 3, 3, 2)) + base
        return one, other

    def build(source, rows, step, one, other):
        shape = (COLS, K3)
        c_one = splat(coefs[step, 0], shape)
        c_other = splat(coefs[step, 1], shape)

        @pl.loop(0, rows)
        def _(i):
            d = [
                c_one * source[one, 2 * i + k] + c_other * source[other, 2 * i + k]
                for k in range(4)
            ]
            for k, value in enumerate(row_transform(d)):
                x_ref[k, pl.ds(pl.multiple_of(i * COLS, COLS), COLS), :] = value

    @pl.loop(0, 8)
    def _(step):
        slot = lax.rem(step, 2)
        tau = lax.rem(step, 4)
        pair = step // 4
        fetch(step, slot).wait()

        @pl.when(step < 7)
        def _():
            fetch(step + 1, 1 - slot).start()

        @pl.when(step == 7)
        def _():
            fetch(step + 1, 1 - slot, u2_hbm).start()

        one, other = frames_of(tau, 2 * pair)
        build(f_ref, I1, step, one, other)
        d = []
        for k in range(4):
            part = pl.ds(k // 2, HALF)
            d.append(
                coefs[step, 0] * h_ref[one, k % 2, part, :]
                + coefs[step, 1] * h_ref[other, k % 2, part, :]
            )
        for k, value in enumerate(row_transform(d)):
            both = jnp.concatenate([value, jnp.zeros((32 - HALF, K3), F32)], axis=0)
            x_ref[k, I1 * COLS :, :] = both.astype(BF)

        @pl.when(tau == 0)
        def _():
            acc_ref[...] = jnp.zeros_like(acc_ref)

        products(step, slot, M1)

        @pl.when(tau == 3)
        def _():
            for member in range(2):
                frame = 2 * pair + member
                for parity in range(2):
                    hn_ref[parity] = norm_act(
                        acc_ref[member, parity, I1 * COLS :, :], g2_ref[...], 1.0
                    )

                @pl.loop(0, I1)
                def _(i):
                    for parity in range(2):
                        row = 2 * i + parity
                        inside = jnp.where(
                            row == 0, top, jnp.where(row == R2 - 1, bottom, 1)
                        ).astype(F32)
                        part = pl.ds(pl.multiple_of(i * COLS, COLS), COLS)
                        value = norm_act(acc_ref[member, parity, part, :], g2_ref[...], inside)
                        a_ref[parity, pl.ds(8, COLS), :] = value
                        a_ref[parity, pl.ds(halo_slot, 1), :] = (
                            hn_ref[parity, pl.ds(i, 1), :] * inside
                        )
                        a_ref[parity, pl.ds(zero_slot, 1), :] = jnp.zeros((1, C), F32)
                        for dx in range(3):
                            s_ref[frame, row, :, dx * C : (dx + 1) * C] = a_ref[
                                parity, pl.ds(7 + dx, COLS), :
                            ].astype(BF)

    acc_ref[...] = jnp.zeros_like(acc_ref)

    @pl.loop(8, 12)
    def _(step):
        slot = lax.rem(step, 2)
        tau = lax.rem(step, 4)
        fetch(step, slot, u2_hbm).wait()

        @pl.when(step < 11)
        def _():
            fetch(step + 1, 1 - slot, u2_hbm).start()

        one, other = frames_of(tau, 0)
        build(s_ref, I2, step, one, other)
        products(step, slot, M2)

    for member in range(2):

        @pl.loop(0, I2)
        def _(i):
            for parity in range(2):
                row = 2 * i + parity
                part = pl.ds(pl.multiple_of(i * COLS, COLS), COLS)
                out_ref[member, row] = (
                    acc_ref[member, parity, part, :] + e_ref[member, row + 2].astype(F32)
                ).astype(BF)


def body(latent, clip_lengths, entry_kernel, first_gain, first_kernel, second_gain, second_kernel):
    tm = lax.axis_index("tm")
    sy = lax.axis_index("sy")
    sx = lax.axis_index("sx")
    start = tm * 2

    earlier = [passed_along(latent, "tm", n) for n in (3, 2, 1)]
    window = padded(jnp.concatenate(earlier + [latent], 0), (("sy", 1), ("sx", 2)), 3)
    u1 = transformed_weights(first_kernel)
    u2 = transformed_weights(second_kernel)

    across = jnp.transpose(window, (1, 3, 0, 2))
    across = jnp.pad(across, ((0, 0), (0, 0), (0, 0), (0, WIDE - 38))).reshape(38 * 16, 8 * WIDE)
    across = jnp.pad(across, ((0, 0), (LEAD + 1 - 3, 384 - 8 * WIDE - (LEAD + 1 - 3))))

    positions = start - 4 + jnp.arange(6, dtype=jnp.int32)
    distance = clip_distance(clip_lengths, positions)
    place = jnp.arange(CELLS)
    frame_of = jnp.clip((place - (LEAD - 4)) // WIDE, 0, 5)
    column_of = place - LEAD - frame_of * WIDE
    pieces = []
    for lag in range(3):
        mask = (distance >= lag)[frame_of].astype(BF)
        for dx in range(3):
            first = (2 - lag) * WIDE + dx
            pieces.append(across[:, first : first + CELLS] * mask[None, :])
    q = jnp.stack(pieces)
    we = jnp.transpose(entry_kernel[::-1], (0, 2, 1, 3, 4)).reshape(432, C)

    low = jnp.where(sx == 0, 0, -2)
    high = jnp.where(sx == 0, COLS + 2, COLS)
    keep = ((column_of >= low) & (column_of < high)).astype(F32)[:, None]

    ints = []
    ints.append(jnp.where(sx == 0, COLS, -1) + LEAD - 1)
    ints.append((sy > 0).astype(jnp.int32))
    ints.append((sy < lax.axis_size("sy") - 1).astype(jnp.int32))
    ints.append(jnp.where(sx == 0, 8 + COLS, 7))
    ints.append(jnp.where(sx == 0, 7, 8 + COLS))
    ints += [0, 0, 0]
    coefs = []
    for pair in (0, 1, 1):
        da = distance[2 + 2 * pair]
        db = distance[3 + 2 * pair]
        k0 = (da >= 2).astype(F32)
        k1 = (da >= 1).astype(F32)
        s = (db >= 1).astype(F32)
        whole = db >= 1
        coefs += [
            [k0, -s, 1.0, 0.0],
            [k1, s, 1.0, s],
            [1.0, -s * k1, 1.0, -s],
            [s * k1, -1.0, 0.0, -1.0],
        ]
        ints += [0, jnp.where(whole, 1, 4), jnp.where(whole, 2, 3), 3]
    ints = jnp.stack([jnp.asarray(v, jnp.int32) for v in ints])
    coefs = jnp.stack([jnp.stack([jnp.asarray(v, F32) for v in line]) for line in coefs])

    vmem = pl.BlockSpec(memory_space=pltpu.VMEM)
    smem = pl.BlockSpec(memory_space=pltpu.SMEM)
    hbm = pl.BlockSpec(memory_space=pl.ANY)
    return pl.pallas_call(
        main_kernel,
        in_specs=[smem, smem, vmem, vmem, vmem, vmem, vmem, hbm, hbm],
        out_specs=vmem,
        out_shape=jax.ShapeDtypeStruct((2, ROWS, COLS, C), BF),
        scratch_shapes=[
            pltpu.VMEM((6, R1, COLS, K3), BF),
            pltpu.VMEM((6, 2, HALF + 8, K3), F32),
            pltpu.VMEM((4, R2, COLS, K3), BF),
            pltpu.VMEM((2, R1, COLS, C), BF),
            pltpu.VMEM((4, M1, K3), BF),
            pltpu.VMEM((4, M1, C), F32),
            pltpu.VMEM((2, 2, M1, C), F32),
            pltpu.VMEM((2, 4, K3, C), BF),
            pltpu.VMEM((ENTRY_ROWS, CELLS, C), F32),
            pltpu.VMEM((ENTRY_ROWS, CELLS, C), F32),
            pltpu.VMEM((2, 32, C), F32),
            pltpu.SemaphoreType.DMA((2,)),
        ],
        compiler_params=pltpu.CompilerParams(vmem_limit_bytes=62 * MIB),
        name="block",
    )(
        ints, coefs, q, we, keep, first_gain[None, :] * 0.5, second_gain[None, :] * 0.5, u1, u2
    )


def solution(mesh):
    return jax.shard_map(
        body,
        mesh=mesh,
        in_specs=(P("tm", "sy", "sx", None), P(), P(), P(), P(), P(), P()),
        out_specs=P("tm", "sy", "sx", None),
        check_vma=False,
    )
```

```python
import functools

import jax
import jax.numpy as jnp
from jax import lax
from jax.experimental import pallas as pl
from jax.experimental.pallas import tpu as pltpu
from jax.sharding import PartitionSpec as P

C = 384
K3 = 3 * C
MIB = 2**20
BF = jnp.bfloat16
F32 = jnp.float32


MESH = pl.DeviceIdType.MESH
ROWS = 32
COLS = 32
HALO = 3
BAND = 16 + 2 * HALO
SOURCES = 4
WEIGHT_STEPS = 9
LAST = 2 * WEIGHT_STEPS - 1
PARTNERS = [(k, d) for k in range(SOURCES) for d in (0, 1, -1) if (k, d) != (0, 0)]
SENT = {0: (0, 16), 1: (16 - HALO, HALO), -1: (0, HALO)}
LANDS = {0: HALO, 1: 0, -1: HALO + 16}
SETS = 14


def weight_block(w_ref, u_ref):
    step = 16

    @pl.loop(0, w_ref.shape[3] // step)
    def _(block):
        part = pl.ds(pl.multiple_of(block * step, step), step)
        w = [[w_ref[t, y, 0, part, :].astype(F32) for y in range(3)] for t in range(3)]
        edge = [w[0][y] + w[2][y] for y in range(3)]
        times = [
            w[0],
            [(edge[y] + w[1][y]) * 0.5 for y in range(3)],
            [(edge[y] - w[1][y]) * 0.5 for y in range(3)],
            w[2],
            w[1],
        ]
        for t, g in enumerate(times):
            outer = g[0] + g[2]
            u_ref[2 * t, 0, part, :] = ((outer + g[1]) * 0.5).astype(BF)
            u_ref[2 * t + 1, 0, part, :] = ((outer - g[1]) * 0.5).astype(BF)
        for n, t in enumerate((1, 2)):
            u_ref[10 + 2 * n, 0, part, :] = times[t][0].astype(BF)
            u_ref[11 + 2 * n, 0, part, :] = times[t][2].astype(BF)


def gather_kernel(
    own_ref, w1_ref, w2_ref, all_ref, u1_ref, u2_ref, send_sem, recv_sem, local_sem, pair_sem
):
    step = pl.program_id(0)
    tm = lax.axis_index("tm")
    sy = lax.axis_index("sy")
    sx = lax.axis_index("sx")
    tms = lax.axis_size("tm")
    sys = lax.axis_size("sy")

    def place(k, d):
        return (lax.rem(tm + k + tms, tms), lax.rem(sy + d + sys, sys), sx)

    def copy(n):
        k, d = PARTNERS[n]
        first, count = SENT[d]
        return pltpu.make_async_remote_copy(
            src_ref=own_ref.at[pl.ds(first, count)],
            dst_ref=all_ref.at[SOURCES - 1 - k, sx, pl.ds(LANDS[d], count)],
            send_sem=send_sem.at[n],
            recv_sem=recv_sem.at[n],
            device_id=place(k, d),
            device_id_type=MESH,
        )

    def local():
        return pltpu.make_async_copy(
            own_ref, all_ref.at[SOURCES - 1, sx, pl.ds(HALO, 16)], local_sem
        )

    def across():
        return pltpu.make_async_remote_copy(
            src_ref=all_ref.at[:, sx],
            dst_ref=all_ref.at[:, sx],
            send_sem=pair_sem.at[0],
            recv_sem=pair_sem.at[1],
            device_id=(tm, sy, 1 - sx),
            device_id_type=MESH,
        )

    @pl.when(step == 0)
    def _():
        barrier = pltpu.get_barrier_semaphore()
        for k, d in PARTNERS:
            pl.semaphore_signal(barrier, inc=1, device_id=place(-k, -d), device_id_type=MESH)
        pl.semaphore_signal(barrier, inc=1, device_id=(tm, sy, 1 - sx), device_id_type=MESH)
        local().start()
        pl.semaphore_wait(barrier, len(PARTNERS) + 1)
        for n in range(len(PARTNERS)):
            copy(n).start()

    @pl.when(step < WEIGHT_STEPS)
    def _():
        weight_block(w1_ref, u1_ref)

    @pl.when(step >= WEIGHT_STEPS)
    def _():
        weight_block(w2_ref, u2_ref)

    @pl.when(step == WEIGHT_STEPS)
    def _():
        local().wait()
        for n in range(len(PARTNERS)):
            copy(n).wait()
        across().start()

    @pl.when(step == LAST)
    def _():
        across().wait()


def gathered(own, first_kernel, second_kernel):
    chunk = C // 3
    hbm = pl.BlockSpec(memory_space=pl.ANY)

    def spec(shape, lead, shift):
        def index(step):
            block = jnp.clip(step - shift, 0, WEIGHT_STEPS - 1)
            return (0,) * lead + (block // 3, block % 3, 0)

        return pl.BlockSpec(shape, index)

    copies = len(PARTNERS)
    sets = jax.ShapeDtypeStruct((SETS, 3, C, C), BF)
    return pl.pallas_call(
        gather_kernel,
        grid=(LAST + 1,),
        in_specs=[
            hbm,
            spec((3, 3, 1, chunk, C), 2, 0),
            spec((3, 3, 1, chunk, C), 2, WEIGHT_STEPS),
        ],
        out_specs=[
            hbm,
            spec((SETS, 1, chunk, C), 1, 0),
            spec((SETS, 1, chunk, C), 1, WEIGHT_STEPS),
        ],
        out_shape=[jax.ShapeDtypeStruct((SOURCES, 2, BAND, 16, 128), BF), sets, sets],
        scratch_shapes=[
            pltpu.SemaphoreType.DMA((copies,)),
            pltpu.SemaphoreType.DMA((copies,)),
            pltpu.SemaphoreType.DMA,
            pltpu.SemaphoreType.DMA((2,)),
        ],
        compiler_params=pltpu.CompilerParams(
            vmem_limit_bytes=62 * MIB, collective_id=0, has_side_effects=True
        ),
        cost_estimate=pl.CostEstimate(
            flops=60 * 9 * C * C, bytes_accessed=2 * 41 * 3 * C * C * 2, transcendentals=0
        ),
        name="gather",
    )(own, first_kernel, second_kernel)


WIDE = 40
LEAD = 9
CELLS = 256
R1 = ROWS + 4
R2 = ROWS + 2
I1 = R2 // 2
I2 = ROWS // 2
M1 = I1 * COLS + 32
M2 = I2 * COLS
HALF = 24
ENTRY_ROWS = 4


def norm_act(values, gain, keep):
    mean = jnp.mean(values * values, axis=-1, keepdims=True)
    half = values * (lax.rsqrt(mean + 1e-6) * keep) * gain
    return half * jnp.tanh(half) + half


def splat(value, shape):
    one = jnp.full((16, 128), value, F32).astype(BF)
    return jnp.tile(one, (shape[0] // 16, shape[1] // 128))


def clip_scalars(lengths, first, count):
    found = [jnp.int32(0)] * count
    start = jnp.int32(0)
    for k in range(lengths.shape[0]):
        for n in range(count):
            t = first + n
            found[n] = jnp.where(start <= t, t - start, found[n])
        start = start + lengths[k]
    return found


def spread_latents(all_ref, q_ref, distance, sx, top, bottom):
    depth = SOURCES * 2 * 128
    index = lax.broadcasted_iota(jnp.int32, (depth, 1), 0)
    source = index // 256
    side = (index // 128) % 2
    half = (index // 64) % 2
    frame = (index // 32) % 2
    x = index % 32
    column = jnp.where(side == sx, x, jnp.where(sx == 0, x + COLS, x - COLS))
    wanted = (column >= -HALO) & (column < COLS + HALO)
    target = (2 * source + frame) * WIDE + column + LEAD + 1
    lane = lax.broadcasted_iota(jnp.int32, (depth, 384), 1)
    spread = []
    for h in range(2):
        to = jnp.where(wanted & (half == h), target, -1)
        pick = jnp.where(lane == to, 1.0, 0.0).astype(BF)
        bands = (0, 16 + HALO) if h else (HALO, BAND)
        rows = (bands[1] - bands[0]) * 16
        lhs = jnp.concatenate(
            [
                all_ref[t, s, bands[0] : bands[1]].reshape(rows, 128)
                for t in range(SOURCES)
                for s in range(2)
            ],
            axis=1,
        )
        spread.append(jnp.dot(lhs, pick, preferred_element_type=F32))
    lower, upper = spread
    edge = HALO * 16
    pt = jnp.concatenate(
        [
            upper[:edge] * top.astype(F32),
            lower[: 16 * 16],
            upper[edge:],
            lower[16 * 16 :] * bottom.astype(F32),
        ],
        axis=0,
    )
    lane = lax.broadcasted_iota(jnp.int32, (1, CELLS), 1)
    frame_of = (lane - (LEAD - 4)) // WIDE
    for lag in range(3):
        keep = jnp.zeros((1, CELLS), F32)
        for f in range(6):
            seen = (distance[f] >= lag).astype(F32)
            keep = jnp.where(frame_of == f, seen, keep)
        for dx in range(3):
            first = (2 - lag) * WIDE + dx
            moved = pltpu.roll(pt, 384 - first, axis=1) if first else pt
            q_ref[3 * lag + dx] = (moved[:, :CELLS] * keep).astype(BF)


def main_kernel(
    lengths, all_ref, we_ref, g1_ref, g2_ref, w1_hbm, w2_hbm, u1_hbm, u2_hbm,
    out_ref,
    q_ref, f_ref, h_ref, s_ref, e_ref, x_ref, m_ref, acc_ref, w_ref, a_ref, b_ref, hn_ref,
    keep_ref, table, coefs, sem,
):
    tm = lax.axis_index("tm")
    sy = lax.axis_index("sy")
    sx = lax.axis_index("sx")
    top = (sy > 0).astype(jnp.int32)
    bottom = (sy < lax.axis_size("sy") - 1).astype(jnp.int32)
    halo_place = jnp.where(sx == 0, COLS, -1) + LEAD - 1
    halo_slot = jnp.where(sx == 0, 8 + COLS, 7)
    zero_slot = jnp.where(sx == 0, 7, 8 + COLS)
    distance = clip_scalars(lengths, 2 * tm - 4, 6)

    for n, pair in enumerate((0, 1, 1)):
        da = distance[2 + 2 * pair]
        whole = distance[3 + 2 * pair] >= 1
        k0 = (da >= 2).astype(F32)
        k1 = (da >= 1).astype(F32)
        s = whole.astype(F32)
        lines = [
            (k0, -s, 1.0, 0.0),
            (k1, s, 1.0, s),
            (1.0, -s * k1, 1.0, -s),
            (s * k1, -1.0, 0.0, -1.0),
        ]
        for tau, line in enumerate(lines):
            for k, value in enumerate(line):
                coefs[4 * n + tau, k] = jnp.float32(value)
        table[4 * n] = 0
        table[4 * n + 1] = jnp.where(whole, 1, 4)
        table[4 * n + 2] = jnp.where(whole, 2, 3)
        table[4 * n + 3] = 3

    def pieces(step, slot, w_hbm, u_hbm):
        which = table[step]
        mixed = pltpu.make_async_copy(
            u_hbm.at[pl.ds(2 * which, 2)], w_ref.at[slot, pl.ds(1, 2)], sem.at[slot, 0]
        )
        tap = jnp.where(which == 0, 0, jnp.where(which == 3, 2, 1))
        time_set = 10 + 2 * jnp.where(which == 2, 1, 0)
        plain = [
            pltpu.make_async_copy(w_hbm.at[tap, 2 * n], w_ref.at[slot, 3 * n], sem.at[slot, 1 + n])
            for n in range(2)
        ]
        made = [
            pltpu.make_async_copy(
                u_hbm.at[time_set + n], w_ref.at[slot, 3 * n], sem.at[slot, 1 + n]
            )
            for n in range(2)
        ]
        return which, mixed, plain, made

    def fetch(step, slot, w_hbm=w1_hbm, u_hbm=u1_hbm):
        which, mixed, plain, made = pieces(step, slot, w_hbm, u_hbm)
        mixed.start()
        time_mixed = (which == 1) | (which == 2)

        @pl.when(time_mixed)
        def _():
            for one in made:
                one.start()

        @pl.when(jnp.logical_not(time_mixed))
        def _():
            for one in plain:
                one.start()

    def arrive(step, slot, w_hbm=w1_hbm, u_hbm=u1_hbm):
        _, mixed, _, made = pieces(step, slot, w_hbm, u_hbm)
        mixed.wait()
        for one in made:
            one.wait()

    fetch(0, 0)
    spread_latents(all_ref, q_ref, distance, sx, top, bottom)
    place = lax.broadcasted_iota(jnp.int32, (CELLS, 128), 0)
    column = place - LEAD - ((place - (LEAD - 4)) // WIDE) * WIDE
    low = jnp.where(sx == 0, 0, -2)
    high = jnp.where(sx == 0, COLS + 2, COLS)
    keep_ref[...] = jnp.where((column >= low) & (column < high), 1.0, 0.0)
    first_gain = g1_ref[...][None, :] * 0.5
    second_gain = g2_ref[...][None, :] * 0.5

    h_ref[...] = jnp.zeros_like(h_ref)

    @pl.loop(0, R1 // ENTRY_ROWS)
    def _(block):
        cols = []
        for n in range(ENTRY_ROWS):
            first = pl.multiple_of((block * ENTRY_ROWS + n) * 16, 16)
            cols.append(
                jnp.concatenate(
                    [
                        q_ref[3 * lag + dx, pl.ds(first + 16 * dy, 16), :]
                        for lag in (2, 1, 0)
                        for dy in range(3)
                        for dx in range(3)
                    ],
                    axis=0,
                )
            )
        patches = jnp.concatenate(cols, axis=1)
        entry = lax.dot_general(
            patches, we_ref[...], (((0,), (0,)), ((), ())), preferred_element_type=F32
        ).astype(BF)
        for n in range(ENTRY_ROWS):
            row = block * ENTRY_ROWS + n
            inside = jnp.where(row < 2, top, jnp.where(row >= R1 - 2, bottom, 1)).astype(F32)
            value = entry[n * CELLS : (n + 1) * CELLS].astype(F32)
            b_ref[n] = value
            a_ref[n] = norm_act(value, first_gain, keep_ref[:, :1] * inside)
        for n in range(ENTRY_ROWS):
            row = block * ENTRY_ROWS + n
            for f in range(2):
                e_ref[f, row] = b_ref[n, pl.ds((4 + f) * WIDE + LEAD, COLS), :].astype(BF)
            for f in range(6):
                for dx in range(3):
                    lanes = slice(dx * C, (dx + 1) * C)
                    place = f * WIDE + LEAD - 1 + dx
                    f_ref[f, row, :, lanes] = a_ref[n, pl.ds(place, COLS), :].astype(BF)
                    h_ref[f, n % 2, pl.ds(row // 2, 1), lanes] = a_ref[
                        n, pl.ds(f * WIDE + halo_place + dx, 1), :
                    ]

    def products(step, slot, rows):
        for k in range(4):
            m_ref[k, :rows, :] = jnp.dot(
                x_ref[k, :rows, :], w_ref[slot, k], preferred_element_type=F32
            )
        first = coefs[step, 2]
        second = coefs[step, 3]

        @pl.loop(0, rows // COLS)
        def _(i):
            part = pl.ds(pl.multiple_of(i * COLS, COLS), COLS)
            terms = [m_ref[k, part, :] for k in range(4)]
            even = terms[0] + terms[1] + terms[2]
            odd = terms[1] - terms[2] - terms[3]
            for parity, value in enumerate((even, odd)):
                acc_ref[0, parity, part, :] += first * value
                acc_ref[1, parity, part, :] += second * value

    def row_transform(d):
        return d[0] - d[2], d[1] + d[2], d[2] - d[1], d[1] - d[3]

    def frames_of(tau, base):
        one = jnp.where(tau == 0, 0, jnp.where(tau == 2, 2, 1)) + base
        other = jnp.where(tau == 2, 1, jnp.where(tau == 3, 3, 2)) + base
        return one, other

    def build(source, rows, step, one, other):
        shape = (COLS, K3)
        c_one = splat(coefs[step, 0], shape)
        c_other = splat(coefs[step, 1], shape)

        @pl.loop(0, rows)
        def _(i):
            d = [
                c_one * source[one, 2 * i + k] + c_other * source[other, 2 * i + k]
                for k in range(4)
            ]
            for k, value in enumerate(row_transform(d)):
                x_ref[k, pl.ds(pl.multiple_of(i * COLS, COLS), COLS), :] = value

    @pl.loop(0, 8)
    def _(step):
        slot = lax.rem(step, 2)
        tau = lax.rem(step, 4)
        pair = step // 4
        arrive(step, slot)

        @pl.when(step < 7)
        def _():
            fetch(step + 1, 1 - slot)

        @pl.when(step == 7)
        def _():
            fetch(step + 1, 1 - slot, w2_hbm, u2_hbm)

        one, other = frames_of(tau, 2 * pair)
        build(f_ref, I1, step, one, other)
        d = []
        for k in range(4):
            part = pl.ds(k // 2, HALF)
            d.append(
                coefs[step, 0] * h_ref[one, k % 2, part, :]
                + coefs[step, 1] * h_ref[other, k % 2, part, :]
            )
        for k, value in enumerate(row_transform(d)):
            both = jnp.concatenate([value, jnp.zeros((32 - HALF, K3), F32)], axis=0)
            x_ref[k, I1 * COLS :, :] = both.astype(BF)

        @pl.when(tau == 0)
        def _():
            acc_ref[...] = jnp.zeros_like(acc_ref)

        products(step, slot, M1)

        @pl.when(tau == 3)
        def _():
            for member in range(2):
                frame = 2 * pair + member
                for parity in range(2):
                    hn_ref[parity] = norm_act(
                        acc_ref[member, parity, I1 * COLS :, :], second_gain, 1.0
                    )

                @pl.loop(0, I1)
                def _(i):
                    for parity in range(2):
                        row = 2 * i + parity
                        inside = jnp.where(
                            row == 0, top, jnp.where(row == R2 - 1, bottom, 1)
                        ).astype(F32)
                        part = pl.ds(pl.multiple_of(i * COLS, COLS), COLS)
                        value = norm_act(acc_ref[member, parity, part, :], second_gain, inside)
                        a_ref[parity, pl.ds(8, COLS), :] = value
                        a_ref[parity, pl.ds(halo_slot, 1), :] = (
                            hn_ref[parity, pl.ds(i, 1), :] * inside
                        )
                        a_ref[parity, pl.ds(zero_slot, 1), :] = jnp.zeros((1, C), F32)
                        for dx in range(3):
                            s_ref[frame, row, :, dx * C : (dx + 1) * C] = a_ref[
                                parity, pl.ds(7 + dx, COLS), :
                            ].astype(BF)

    acc_ref[...] = jnp.zeros_like(acc_ref)

    @pl.loop(8, 12)
    def _(step):
        slot = lax.rem(step, 2)
        tau = lax.rem(step, 4)
        arrive(step, slot, w2_hbm, u2_hbm)

        @pl.when(step < 11)
        def _():
            fetch(step + 1, 1 - slot, w2_hbm, u2_hbm)

        one, other = frames_of(tau, 0)
        build(s_ref, I2, step, one, other)
        products(step, slot, M2)

    for member in range(2):

        @pl.loop(0, I2)
        def _(i):
            for parity in range(2):
                row = 2 * i + parity
                part = pl.ds(pl.multiple_of(i * COLS, COLS), COLS)
                out_ref[member, row] = (
                    acc_ref[member, parity, part, :] + e_ref[member, row + 2].astype(F32)
                ).astype(BF)


def block_call(*operands):
    vmem = pl.BlockSpec(memory_space=pltpu.VMEM)
    smem = pl.BlockSpec(memory_space=pltpu.SMEM)
    hbm = pl.BlockSpec(memory_space=pl.ANY)
    return pl.pallas_call(
        main_kernel,
        in_specs=[smem, vmem, vmem, vmem, vmem, hbm, hbm, hbm, hbm],
        out_specs=vmem,
        out_shape=jax.ShapeDtypeStruct((2, ROWS, COLS, C), BF),
        scratch_shapes=[
            pltpu.VMEM((9, 38 * 16, CELLS), BF),
            pltpu.VMEM((6, R1, COLS, K3), BF),
            pltpu.VMEM((6, 2, HALF + 8, K3), F32),
            pltpu.VMEM((4, R2, COLS, K3), BF),
            pltpu.VMEM((2, R1, COLS, C), BF),
            pltpu.VMEM((4, M1, K3), BF),
            pltpu.VMEM((4, M1, C), F32),
            pltpu.VMEM((2, 2, M1, C), F32),
            pltpu.VMEM((2, 4, K3, C), BF),
            pltpu.VMEM((ENTRY_ROWS, CELLS, C), F32),
            pltpu.VMEM((ENTRY_ROWS, CELLS, C), F32),
            pltpu.VMEM((2, 32, C), F32),
            pltpu.VMEM((CELLS, 128), F32),
            pltpu.SMEM((12,), jnp.int32),
            pltpu.SMEM((12, 4), F32),
            pltpu.SemaphoreType.DMA((2, 3)),
        ],
        compiler_params=pltpu.CompilerParams(vmem_limit_bytes=62 * MIB),
        name="block",
    )(*operands)


def body(latent, clip_lengths, entry_kernel, first_gain, first_kernel, second_gain, second_kernel):
    own = latent.reshape(2, 2, 16, COLS, 16).transpose(2, 4, 1, 0, 3).reshape(16, 16, 128)
    everything, u1, u2 = gathered(own, first_kernel, second_kernel)
    return block_call(
        clip_lengths,
        everything,
        entry_kernel.reshape(27 * 16, C),
        first_gain,
        second_gain,
        first_kernel.reshape(3, 3, K3, C),
        second_kernel.reshape(3, 3, K3, C),
        u1.reshape(SETS, K3, C),
        u2.reshape(SETS, K3, C),
    )


def solution(mesh):
    return jax.shard_map(
        body,
        mesh=mesh,
        in_specs=(P("tm", "sy", "sx", None), P(), P(), P(), P(), P(), P()),
        out_specs=P("tm", "sy", "sx", None),
        check_vma=False,
    )
```

```python
import functools

import jax
import jax.numpy as jnp
from jax import lax
from jax.experimental import pallas as pl
from jax.experimental.pallas import tpu as pltpu
from jax.sharding import PartitionSpec as P

C = 384
K3 = 3 * C
MIB = 2**20
BF = jnp.bfloat16
F32 = jnp.float32


MESH = pl.DeviceIdType.MESH
ROWS = 32
COLS = 32
HALO = 3
BAND = 16 + 2 * HALO
SOURCES = 4
WEIGHT_STEPS = 9
LAST = 2 * WEIGHT_STEPS - 1
PARTNERS = [(k, d) for k in range(SOURCES) for d in (0, 1, -1) if (k, d) != (0, 0)]
SENT = {0: (0, 16), 1: (16 - HALO, HALO), -1: (0, HALO)}
LANDS = {0: HALO, 1: 0, -1: HALO + 16}
SETS = 14
ENTERED = 2


def weight_block(w_ref, u_ref):
    step = 16

    @pl.loop(0, w_ref.shape[3] // step)
    def _(block):
        part = pl.ds(pl.multiple_of(block * step, step), step)
        w = [[w_ref[t, y, 0, part, :].astype(F32) for y in range(3)] for t in range(3)]
        edge = [w[0][y] + w[2][y] for y in range(3)]
        times = [
            w[0],
            [(edge[y] + w[1][y]) * 0.5 for y in range(3)],
            [(edge[y] - w[1][y]) * 0.5 for y in range(3)],
            w[2],
            w[1],
        ]
        for t, g in enumerate(times):
            outer = g[0] + g[2]
            u_ref[2 * t, 0, part, :] = ((outer + g[1]) * 0.5).astype(BF)
            u_ref[2 * t + 1, 0, part, :] = ((outer - g[1]) * 0.5).astype(BF)
        for n, t in enumerate((1, 2)):
            u_ref[10 + 2 * n, 0, part, :] = times[t][0].astype(BF)
            u_ref[11 + 2 * n, 0, part, :] = times[t][2].astype(BF)


def gather_kernel(
    own_ref, w1_ref, w2_ref, all_ref, u1_ref, u2_ref, send_sem, recv_sem, local_sem, pair_sem
):
    step = pl.program_id(0)
    tm = lax.axis_index("tm")
    sy = lax.axis_index("sy")
    sx = lax.axis_index("sx")
    tms = lax.axis_size("tm")
    sys = lax.axis_size("sy")

    def place(k, d):
        return (lax.rem(tm + k + tms, tms), lax.rem(sy + d + sys, sys), sx)

    def copy(n):
        k, d = PARTNERS[n]
        first, count = SENT[d]
        return pltpu.make_async_remote_copy(
            src_ref=own_ref.at[pl.ds(first, count)],
            dst_ref=all_ref.at[SOURCES - 1 - k, sx, pl.ds(LANDS[d], count)],
            send_sem=send_sem.at[n],
            recv_sem=recv_sem.at[n],
            device_id=place(k, d),
            device_id_type=MESH,
        )

    def local():
        return pltpu.make_async_copy(
            own_ref, all_ref.at[SOURCES - 1, sx, pl.ds(HALO, 16)], local_sem
        )

    def across():
        return pltpu.make_async_remote_copy(
            src_ref=all_ref.at[:, sx],
            dst_ref=all_ref.at[:, sx],
            send_sem=pair_sem.at[0],
            recv_sem=pair_sem.at[1],
            device_id=(tm, sy, 1 - sx),
            device_id_type=MESH,
        )

    @pl.when(step == 0)
    def _():
        barrier = pltpu.get_barrier_semaphore()
        for k, d in PARTNERS:
            pl.semaphore_signal(barrier, inc=1, device_id=place(-k, -d), device_id_type=MESH)
        pl.semaphore_signal(barrier, inc=1, device_id=(tm, sy, 1 - sx), device_id_type=MESH)
        local().start()

    @pl.when(step == ENTERED)
    def _():
        pl.semaphore_wait(pltpu.get_barrier_semaphore(), len(PARTNERS) + 1)
        for n in range(len(PARTNERS)):
            copy(n).start()

    @pl.when(step < WEIGHT_STEPS)
    def _():
        weight_block(w1_ref, u1_ref)

    @pl.when(step >= WEIGHT_STEPS)
    def _():
        weight_block(w2_ref, u2_ref)

    @pl.when(step == WEIGHT_STEPS)
    def _():
        local().wait()
        for n in range(len(PARTNERS)):
            copy(n).wait()
        across().start()

    @pl.when(step == LAST)
    def _():
        across().wait()


def gathered(own, first_kernel, second_kernel):
    chunk = C // 3
    hbm = pl.BlockSpec(memory_space=pl.ANY)

    def spec(shape, lead, shift):
        def index(step):
            block = jnp.clip(step - shift, 0, WEIGHT_STEPS - 1)
            return (0,) * lead + (block // 3, block % 3, 0)

        return pl.BlockSpec(shape, index)

    copies = len(PARTNERS)
    sets = jax.ShapeDtypeStruct((SETS, 3, C, C), BF)
    return pl.pallas_call(
        gather_kernel,
        grid=(LAST + 1,),
        in_specs=[
            hbm,
            spec((3, 3, 1, chunk, C), 2, 0),
            spec((3, 3, 1, chunk, C), 2, WEIGHT_STEPS),
        ],
        out_specs=[
            hbm,
            spec((SETS, 1, chunk, C), 1, 0),
            spec((SETS, 1, chunk, C), 1, WEIGHT_STEPS),
        ],
        out_shape=[jax.ShapeDtypeStruct((SOURCES, 2, BAND, 16, 128), BF), sets, sets],
        scratch_shapes=[
            pltpu.SemaphoreType.DMA((copies,)),
            pltpu.SemaphoreType.DMA((copies,)),
            pltpu.SemaphoreType.DMA,
            pltpu.SemaphoreType.DMA((2,)),
        ],
        compiler_params=pltpu.CompilerParams(
            vmem_limit_bytes=62 * MIB, collective_id=0, has_side_effects=True
        ),
        cost_estimate=pl.CostEstimate(
            flops=60 * 9 * C * C, bytes_accessed=2 * 41 * 3 * C * C * 2, transcendentals=0
        ),
        name="gather",
    )(own, first_kernel, second_kernel)


WIDE = 40
LEAD = 9
SPAN = 16
CELLS = 256
USED = 6 * 2 * SPAN + 24
INNER = 6 * 2 * SPAN
R1 = ROWS + 4
R2 = ROWS + 2
I1 = R2 // 2
I2 = ROWS // 2
HALO_ROWS = 32
ENTRY_ROWS = 4
QUARTER = 4


def norm_act(values, gain, keep):
    mean = jnp.mean(values * values, axis=-1, keepdims=True)
    half = values * (lax.rsqrt(mean + 1e-6) * keep) * gain
    return half * jnp.tanh(half) + half


def shifted(values, edge, ahead):
    line = lax.broadcasted_iota(jnp.int32, values.shape, 0)
    if ahead:
        return jnp.where(line == SPAN - 1, edge, pltpu.roll(values, SPAN - 1, axis=0))
    return jnp.where(line == 0, edge, pltpu.roll(values, 1, axis=0))


def clip_scalars(lengths, first, count):
    found = [jnp.int32(0)] * count
    start = jnp.int32(0)
    for k in range(lengths.shape[0]):
        for n in range(count):
            t = first + n
            found[n] = jnp.where(start <= t, t - start, found[n])
        start = start + lengths[k]
    return found


def spread_latents(all_ref, q_ref, distance, sx, top, bottom):
    depth = SOURCES * 2 * 128
    index = lax.broadcasted_iota(jnp.int32, (depth, 1), 0)
    source = index // 256
    side = (index // 128) % 2
    half = (index // 64) % 2
    frame = (index // 32) % 2
    x = index % 32
    column = jnp.where(side == sx, x, jnp.where(sx == 0, x + COLS, x - COLS))
    wanted = (column >= -HALO) & (column < COLS + HALO)
    target = (2 * source + frame) * WIDE + column + LEAD + 1
    lane = lax.broadcasted_iota(jnp.int32, (depth, 384), 1)
    spread = []
    for h in range(2):
        to = jnp.where(wanted & (half == h), target, -1)
        pick = jnp.where(lane == to, 1.0, 0.0).astype(BF)
        bands = (0, 16 + HALO) if h else (HALO, BAND)
        rows = (bands[1] - bands[0]) * 16
        lhs = jnp.concatenate(
            [
                all_ref[t, s, bands[0] : bands[1]].reshape(rows, 128)
                for t in range(SOURCES)
                for s in range(2)
            ],
            axis=1,
        )
        spread.append(jnp.dot(lhs, pick, preferred_element_type=F32))
    lower, upper = spread
    edge = HALO * 16
    pt = jnp.concatenate(
        [
            upper[:edge] * top.astype(F32),
            lower[: 16 * 16],
            upper[edge:],
            lower[16 * 16 :] * bottom.astype(F32),
        ],
        axis=0,
    )
    pt = pt.astype(BF)
    cell = lax.broadcasted_iota(jnp.int32, (1, CELLS), 1)
    beyond = cell - INNER
    halo = beyond // 6
    frame_of = jnp.where(cell < INNER, cell // 32, beyond - 6 * halo)
    column = jnp.where(
        cell < INNER,
        2 * (cell % SPAN) + (cell // SPAN) % 2,
        jnp.where(halo < 2, halo - 2, COLS + halo - 2),
    )
    base = frame_of * WIDE + column + LEAD
    line = lax.broadcasted_iota(jnp.int32, (384, CELLS), 0)
    for lag in range(3):
        keep = jnp.zeros((1, CELLS), jnp.int32)
        for f in range(6):
            keep = jnp.where(frame_of == f, (distance[f] >= lag).astype(jnp.int32), keep)
        keep = jnp.where(cell < USED, keep, 0)
        for dx in range(3):
            to = jnp.where(keep == 1, base + (2 - lag) * WIDE + dx, -1)
            pick = jnp.where(line == to, 1.0, 0.0).astype(BF)
            q_ref[3 * lag + dx] = jnp.dot(pt, pick, preferred_element_type=F32).astype(BF)


def main_kernel(
    lengths, all_ref, we_ref, g1_ref, g2_ref, w1_hbm, w2_hbm, u1_hbm, u2_hbm,
    out_ref,
    q_ref, f_ref, h_ref, s_ref, e_ref, xa_ref, xb_ref, hxa_ref, hxb_ref, ma_ref, mb_ref, acc_ref,
    w_ref, a_ref, b_ref, hn_ref, keep_ref, sem,
):
    tm = lax.axis_index("tm")
    sy = lax.axis_index("sy")
    sx = lax.axis_index("sx")
    top = (sy > 0).astype(jnp.int32)
    bottom = (sy < lax.axis_size("sy") - 1).astype(jnp.int32)
    left = sx == 0
    distance = clip_scalars(lengths, 2 * tm - 4, 6)
    x_refs, hx_refs, m_refs = (xa_ref, xb_ref), (hxa_ref, hxb_ref), (ma_ref, mb_ref)

    def pair_of(step):
        n = (0, 1, 1)[step // 4]
        whole = distance[3 + 2 * n] >= 1
        return (
            (distance[2 + 2 * n] >= 2).astype(F32),
            (distance[2 + 2 * n] >= 1).astype(F32),
            whole.astype(F32),
            whole,
        )

    def weight_copies(step):
        slot, tau = step % 2, step % 4
        w_hbm, u_hbm = (w1_hbm, u1_hbm) if step < 8 else (w2_hbm, u2_hbm)
        whole = pair_of(step)[3]
        which = (0, jnp.where(whole, 1, 4), jnp.where(whole, 2, 3), 3)[tau]
        mixed = pltpu.make_async_copy(
            u_hbm.at[pl.ds(2 * which, 2)], w_ref.at[slot, pl.ds(1, 2)], sem.at[slot, 0]
        )

        def outer(source, n):
            return pltpu.make_async_copy(source, w_ref.at[slot, 3 * n], sem.at[slot, 1 + n])

        tap = (0, 1, 2, 2)[tau]
        plain = [outer(w_hbm.at[tap, 2 * n], n) for n in range(2)]
        made = None
        if tau in (1, 2):
            made = [outer(u_hbm.at[8 + 2 * tau + n], n) for n in range(2)]
        return whole, mixed, plain, made

    def fetch(step):
        whole, mixed, plain, made = weight_copies(step)
        mixed.start()
        if made is None:
            for one in plain:
                one.start()
            return

        @pl.when(whole)
        def _():
            for one in made:
                one.start()

        @pl.when(jnp.logical_not(whole))
        def _():
            for one in plain:
                one.start()

    def arrive(step):
        _, mixed, plain, _ = weight_copies(step)
        mixed.wait()
        for one in plain:
            one.wait()

    fetch(0)
    spread_latents(all_ref, q_ref, distance, sx, top, bottom)
    cell = lax.broadcasted_iota(jnp.int32, (USED, 128), 0)
    off_left = (cell >= INNER) & (cell < INNER + 12)
    off_right = cell >= INNER + 12
    keep_ref[...] = jnp.where((off_left & left) | (off_right & (sx == 1)), 0.0, 1.0)
    first_gain = g1_ref[...][None, :] * 0.5
    second_gain = g2_ref[...][None, :] * 0.5
    h_ref[...] = jnp.zeros_like(h_ref)

    @pl.loop(0, R1 // ENTRY_ROWS)
    def _(block):
        cols = []
        for n in range(ENTRY_ROWS):
            first = pl.multiple_of((block * ENTRY_ROWS + n) * 16, 16)
            cols.append(
                jnp.concatenate(
                    [
                        q_ref[3 * lag + dx, pl.ds(first + 16 * dy, 16), :]
                        for lag in (2, 1, 0)
                        for dy in range(3)
                        for dx in range(3)
                    ],
                    axis=0,
                )
            )
        patches = jnp.concatenate(cols, axis=1)
        entry = lax.dot_general(
            patches, we_ref[...], (((0,), (0,)), ((), ())), preferred_element_type=F32
        ).astype(BF)
        for n in range(ENTRY_ROWS):
            row = block * ENTRY_ROWS + n
            inside = jnp.where(row < 2, top, jnp.where(row >= R1 - 2, bottom, 1)).astype(F32)
            value = entry[n * CELLS : n * CELLS + USED].astype(F32)
            for f in range(2):
                e_ref[f, row] = entry[n * CELLS + (4 + f) * 32 : n * CELLS + (5 + f) * 32]
            a_ref[n] = norm_act(value, first_gain, keep_ref[:, :1] * inside)
        for n in range(ENTRY_ROWS):
            row = block * ENTRY_ROWS + n
            for f in range(6):
                even = a_ref[n, f * 32 : f * 32 + SPAN, :]
                odd = a_ref[n, f * 32 + SPAN : f * 32 + 2 * SPAN, :]
                before = a_ref[n, INNER + 6 + f : INNER + 7 + f, :]
                after = a_ref[n, INNER + 12 + f : INNER + 13 + f, :]
                f_ref[f, row, 0] = shifted(odd, before, False).astype(BF)
                f_ref[f, row, 1] = even.astype(BF)
                f_ref[f, row, 2] = odd.astype(BF)
                f_ref[f, row, 3] = shifted(even, after, True).astype(BF)
                places = (
                    jnp.where(left, f * 32 + 31, INNER + f),
                    jnp.where(left, INNER + 12 + f, INNER + 6 + f),
                    jnp.where(left, INNER + 18 + f, f * 32),
                )
                for dx, place in enumerate(places):
                    h_ref[f, n % 2, pl.ds(row // 2, 1), dx * C : (dx + 1) * C] = a_ref[
                        n, pl.ds(place, 1), :
                    ]

    def time_mix(step, one, dtype):
        tau = step % 4
        k0, k1, s, _ = pair_of(step)
        base = 2 if 4 <= step < 8 else 0

        def scaled(value, by):
            if dtype == F32:
                return value * by
            tile = jnp.full((16, 128), by, F32).astype(BF)
            return value * jnp.tile(tile, (1, value.shape[1] // 128))

        if tau == 0:
            return scaled(one(base), k0) - scaled(one(base + 2), s)
        if tau == 1:
            return scaled(one(base + 1), k1) + scaled(one(base + 2), s)
        if tau == 2:
            return one(base + 2) - scaled(one(base + 1), s * k1)
        return scaled(one(base + 1), s * k1) - one(base + 3)

    def row_transform(d):
        return d[0] - d[2], d[1] + d[2], d[2] - d[1], d[1] - d[3]

    def build(step, i):
        source = f_ref if step < 8 else s_ref
        x_ref = x_refs[step % 2]
        for j in range(4):
            d = [
                time_mix(step, lambda frame, k=k: source[frame, 2 * i + k, j], BF)
                for k in range(4)
            ]
            for k, value in enumerate(row_transform(d)):
                x_ref[k, j, pl.ds(pl.multiple_of(i * SPAN, SPAN), SPAN), :] = value

    def build_halo(step):
        hx_ref = hx_refs[step % 2]
        for dx in range(3):
            lanes = slice(dx * C, (dx + 1) * C)
            d = [
                time_mix(
                    step,
                    lambda frame, k=k: h_ref[frame, k % 2, pl.ds(k // 2, HALO_ROWS), lanes],
                    F32,
                )
                for k in range(4)
            ]
            for k, value in enumerate(row_transform(d)):
                hx_ref[k, :, lanes] = value.astype(BF)

    def settle(step, part):
        tau = step % 4
        m_ref = m_refs[step % 2]
        s = pair_of(step)[2]
        t = [m_ref[k, part, :] for k in range(4)]
        middle = t[1] - t[2]
        both = (t[0] + t[1] + t[2], middle - t[3])
        if tau == 3:
            return 1, [acc_ref[1, p, part, :] - both[p] for p in range(2)]
        if tau == 2:
            for p in range(2):
                acc_ref[1, p, part, :] = acc_ref[1, p, part, :] - s * both[p]
            return 0, [acc_ref[0, p, part, :] + both[p] for p in range(2)]
        for p in range(2):
            if tau == 0:
                acc_ref[0, p, part, :] = both[p]
            else:
                acc_ref[0, p, part, :] = acc_ref[0, p, part, :] + both[p]
                acc_ref[1, p, part, :] = s * both[p]
        return None

    def settle_halo(step):
        done = settle(step, pl.ds(2 * I1 * SPAN, HALO_ROWS))
        if done is not None:
            for p, value in enumerate(done[1]):
                hn_ref[p] = norm_act(value, second_gain, 1.0)

    def settle_first(step, i):
        for side in range(2):
            first = pl.multiple_of(side * I1 * SPAN + i * SPAN, SPAN)
            done = settle(step, pl.ds(first, SPAN))
            if done is None:
                continue
            frame = 2 * (step // 4) + done[0]
            for p, value in enumerate(done[1]):
                row = 2 * i + p
                inside = jnp.where(row == 0, top, jnp.where(row == R2 - 1, bottom, 1)).astype(F32)
                value = norm_act(value, second_gain, inside)
                here = inside * jnp.where(sx == side, 1.0, 0.0)
                edge = hn_ref[p, pl.ds(i, 1), :] * here
                if side == 0:
                    s_ref[frame, row, 1] = value.astype(BF)
                    s_ref[frame, row, 3] = shifted(value, edge, True).astype(BF)
                else:
                    s_ref[frame, row, 2] = value.astype(BF)
                    s_ref[frame, row, 0] = shifted(value, edge, False).astype(BF)

    def settle_second(step, i, n):
        done = [
            settle(step, pl.ds(pl.multiple_of(side * I2 * SPAN + i * SPAN, SPAN), SPAN))
            for side in range(2)
        ]
        if done[0] is None:
            return
        member = done[0][0]
        for p in range(2):
            row = 2 * i + p
            for side in range(2):
                part = slice(side * SPAN, (side + 1) * SPAN)
                value = done[side][1][p] + e_ref[member, row + 2, part, :].astype(F32)
                for lane in range(3):
                    b_ref[2 * n + p, lane, pl.ds(side, SPAN, stride=2), :] = value[
                        :, lane * 128 : (lane + 1) * 128
                    ]
            for lane in range(3):
                out_ref[member, row, :, lane * 128 : (lane + 1) * 128] = b_ref[
                    2 * n + p, lane
                ].astype(BF)

    def products(step, k):
        x_ref, m_ref = x_refs[step % 2], m_refs[step % 2]
        count = (I1 if step < 8 else I2) * SPAN
        x = [x_ref[k, j, :count, :] for j in range(4)]
        parts = [jnp.concatenate(x[:3], axis=1), jnp.concatenate(x[1:], axis=1)]
        if step < 8:
            parts.append(hx_refs[step % 2][k])
        lhs = jnp.concatenate(parts, axis=0)
        m_ref[k, : lhs.shape[0], :] = jnp.dot(
            lhs, w_ref[step % 2, k], preferred_element_type=F32
        )

    def build_alone(step):
        @pl.loop(0, I1 if step < 8 else I2)
        def _(i):
            build(step, i)

        if step < 8:
            build_halo(step)

    def run(step):
        arrive(step)
        if step < 11:
            fetch(step + 1)
        builds = step not in (7, 11)
        settles = step not in (0, 8)
        if builds and step < 8:
            build(step + 1, I1 - 1)
            build_halo(step + 1)
        if settles and step < 8:
            settle_halo(step - 1)
            settle_first(step - 1, I1 - 1)

        @pl.loop(0, 4)
        def _(k):
            products(step, k)
            for n in range(QUARTER):
                i = QUARTER * k + n
                if builds:
                    build(step + 1, i)
                if settles:
                    if step < 8:
                        settle_first(step - 1, i)
                    else:
                        settle_second(step - 1, i, n)

    build_alone(0)
    for step in range(8):
        run(step)
    settle_halo(7)

    @pl.loop(0, I1)
    def _(i):
        settle_first(7, i)

    build_alone(8)
    for step in range(8, 12):
        run(step)

    @pl.loop(0, 4)
    def _(k):
        for n in range(QUARTER):
            settle_second(11, QUARTER * k + n, n)


def block_call(*operands):
    vmem = pl.BlockSpec(memory_space=pltpu.VMEM)
    smem = pl.BlockSpec(memory_space=pltpu.SMEM)
    hbm = pl.BlockSpec(memory_space=pl.ANY)
    m1 = 2 * I1 * SPAN + HALO_ROWS
    return pl.pallas_call(
        main_kernel,
        in_specs=[smem, vmem, vmem, vmem, vmem, hbm, hbm, hbm, hbm],
        out_specs=vmem,
        out_shape=jax.ShapeDtypeStruct((2, ROWS, COLS, C), BF),
        scratch_shapes=[
            pltpu.VMEM((9, 38 * 16, CELLS), BF),
            pltpu.VMEM((6, R1, 4, SPAN, C), BF),
            pltpu.VMEM((6, 2, HALO_ROWS + 8, K3), F32),
            pltpu.VMEM((4, R2, 4, SPAN, C), BF),
            pltpu.VMEM((2, R1, COLS, C), BF),
            pltpu.VMEM((4, 4, I1 * SPAN, C), BF),
            pltpu.VMEM((4, 4, I1 * SPAN, C), BF),
            pltpu.VMEM((4, HALO_ROWS, K3), BF),
            pltpu.VMEM((4, HALO_ROWS, K3), BF),
            pltpu.VMEM((4, m1, C), F32),
            pltpu.VMEM((4, m1, C), F32),
            pltpu.VMEM((2, 2, m1, C), F32),
            pltpu.VMEM((2, 4, K3, C), BF),
            pltpu.VMEM((ENTRY_ROWS, USED, C), F32),
            pltpu.VMEM((2 * QUARTER, 3, COLS, 128), F32),
            pltpu.VMEM((2, HALO_ROWS, C), F32),
            pltpu.VMEM((USED, 128), F32),
            pltpu.SemaphoreType.DMA((2, 3)),
        ],
        compiler_params=pltpu.CompilerParams(vmem_limit_bytes=62 * MIB),
        name="block",
    )(*operands)


def body(latent, clip_lengths, entry_kernel, first_gain, first_kernel, second_gain, second_kernel):
    own = latent.reshape(2, 2, 16, COLS, 16).transpose(2, 4, 1, 0, 3).reshape(16, 16, 128)
    everything, u1, u2 = gathered(own, first_kernel, second_kernel)
    return block_call(
        clip_lengths,
        everything,
        entry_kernel.reshape(27 * 16, C),
        first_gain,
        second_gain,
        first_kernel.reshape(3, 3, K3, C),
        second_kernel.reshape(3, 3, K3, C),
        u1.reshape(SETS, K3, C),
        u2.reshape(SETS, K3, C),
    )


def solution(mesh):
    return jax.shard_map(
        body,
        mesh=mesh,
        in_specs=(P("tm", "sy", "sx", None), P(), P(), P(), P(), P(), P()),
        out_specs=P("tm", "sy", "sx", None),
        check_vma=False,
    )
```

```python
import functools

import jax
import jax.numpy as jnp
from jax import lax
from jax.experimental import pallas as pl
from jax.experimental.pallas import tpu as pltpu
from jax.sharding import PartitionSpec as P

C = 384
K3 = 3 * C
MIB = 2**20
BF = jnp.bfloat16
F32 = jnp.float32


MESH = pl.DeviceIdType.MESH
ROWS = 32
COLS = 32
HALO = 3
BAND = 16 + 2 * HALO
SOURCES = 4
WEIGHT_STEPS = 9
LAST = WEIGHT_STEPS - 1
PARTNERS = [(k, d) for k in range(SOURCES) for d in (0, 1, -1) if (k, d) != (0, 0)]
SENT = {0: (0, 16), 1: (16 - HALO, HALO), -1: (0, HALO)}
LANDS = {0: HALO, 1: 0, -1: HALO + 16}
SETS = 14
ENTERED = 1
LANDED = 5


def mix_weights(w, put):
    edge = [w[0][y] + w[2][y] for y in range(3)]
    times = [
        w[0],
        [(edge[y] + w[1][y]) * 0.5 for y in range(3)],
        [(edge[y] - w[1][y]) * 0.5 for y in range(3)],
        w[2],
        w[1],
    ]
    for t, g in enumerate(times):
        outer = g[0] + g[2]
        put(2 * t, (outer + g[1]) * 0.5)
        put(2 * t + 1, (outer - g[1]) * 0.5)
    for n, t in enumerate((1, 2)):
        put(10 + 2 * n, times[t][0])
        put(11 + 2 * n, times[t][2])


def weight_block(w_ref, u_ref):
    step = 16

    @pl.loop(0, w_ref.shape[3] // step)
    def _(block):
        part = pl.ds(pl.multiple_of(block * step, step), step)
        for lane in range(3):
            lanes = slice(lane * 128, (lane + 1) * 128)
            w = [[w_ref[t, y, 0, part, lanes].astype(F32) for y in range(3)] for t in range(3)]

            def put(n, value, lanes=lanes):
                u_ref[n, 0, part, lanes] = value.astype(BF)

            mix_weights(w, put)


def gather_kernel(
    own_ref, w1_ref, all_ref, u1_ref, send_sem, recv_sem, local_sem, pair_sem
):
    step = pl.program_id(0)
    tm = lax.axis_index("tm")
    sy = lax.axis_index("sy")
    sx = lax.axis_index("sx")
    tms = lax.axis_size("tm")
    sys = lax.axis_size("sy")

    def place(k, d):
        return (lax.rem(tm + k + tms, tms), lax.rem(sy + d + sys, sys), sx)

    def copy(n):
        k, d = PARTNERS[n]
        first, count = SENT[d]
        return pltpu.make_async_remote_copy(
            src_ref=own_ref.at[pl.ds(first, count)],
            dst_ref=all_ref.at[SOURCES - 1 - k, sx, pl.ds(LANDS[d], count)],
            send_sem=send_sem.at[n],
            recv_sem=recv_sem.at[n],
            device_id=place(k, d),
            device_id_type=MESH,
        )

    def local():
        return pltpu.make_async_copy(
            own_ref, all_ref.at[SOURCES - 1, sx, pl.ds(HALO, 16)], local_sem
        )

    def across():
        return pltpu.make_async_remote_copy(
            src_ref=all_ref.at[:, sx],
            dst_ref=all_ref.at[:, sx],
            send_sem=pair_sem.at[0],
            recv_sem=pair_sem.at[1],
            device_id=(tm, sy, 1 - sx),
            device_id_type=MESH,
        )

    @pl.when(step == 0)
    def _():
        barrier = pltpu.get_barrier_semaphore()
        for k, d in PARTNERS:
            pl.semaphore_signal(barrier, inc=1, device_id=place(-k, -d), device_id_type=MESH)
        pl.semaphore_signal(barrier, inc=1, device_id=(tm, sy, 1 - sx), device_id_type=MESH)
        local().start()

    @pl.when(step == ENTERED)
    def _():
        pl.semaphore_wait(pltpu.get_barrier_semaphore(), len(PARTNERS) + 1)
        for n in range(len(PARTNERS)):
            copy(n).start()

    weight_block(w1_ref, u1_ref)

    @pl.when(step == LANDED)
    def _():
        local().wait()
        for n in range(len(PARTNERS)):
            copy(n).wait()
        across().start()

    @pl.when(step == LAST)
    def _():
        across().wait()


def gathered(own, first_kernel):
    chunk = C // 3
    hbm = pl.BlockSpec(memory_space=pl.ANY)
    copies = len(PARTNERS)
    return pl.pallas_call(
        gather_kernel,
        grid=(WEIGHT_STEPS,),
        in_specs=[
            hbm,
            pl.BlockSpec((3, 3, 1, chunk, C), lambda step: (0, 0, step // 3, step % 3, 0)),
        ],
        out_specs=[
            hbm,
            pl.BlockSpec((SETS, 1, chunk, C), lambda step: (0, step // 3, step % 3, 0)),
        ],
        out_shape=[
            jax.ShapeDtypeStruct((SOURCES, 2, BAND, 16, 128), BF),
            jax.ShapeDtypeStruct((SETS, 3, C, C), BF),
        ],
        scratch_shapes=[
            pltpu.SemaphoreType.DMA((copies,)),
            pltpu.SemaphoreType.DMA((copies,)),
            pltpu.SemaphoreType.DMA,
            pltpu.SemaphoreType.DMA((2,)),
        ],
        compiler_params=pltpu.CompilerParams(
            vmem_limit_bytes=62 * MIB, collective_id=0, has_side_effects=True
        ),
        cost_estimate=pl.CostEstimate(
            flops=60 * 9 * C * C, bytes_accessed=41 * 3 * C * C * 2, transcendentals=0
        ),
        name="gather",
    )(own, first_kernel)


WIDE = 40
LEAD = 9
SPAN = 16
CELLS = 256
USED = 6 * 2 * SPAN + 24
INNER = 6 * 2 * SPAN
R1 = ROWS + 4
R2 = ROWS + 2
I1 = R2 // 2
I2 = ROWS // 2
HALO_ROWS = 32
ENTRY_ROWS = 4
QUARTER = 4
QUARTERS = 4
PIECE = 48
PIECES = K3 // PIECE
AHEAD = 3


def norm_act(values, gain, keep):
    mean = jnp.mean(values * values, axis=-1, keepdims=True)
    half = values * (lax.rsqrt(mean + 1e-6) * keep) * gain
    return half * jnp.tanh(half) + half


def norm_act_wide(values, gain, keep):
    squares = values * values
    folded = squares[:, :128] + squares[:, 128:256] + squares[:, 256:]
    ones = jnp.full((128, 128), 1.0, BF)
    mean = jnp.dot(folded.astype(BF), ones, preferred_element_type=F32) * (1.0 / C)
    scale = lax.rsqrt(mean + 1e-6) * keep
    half = values * jnp.concatenate([scale] * 3, axis=1) * gain
    return half * jnp.tanh(half) + half


def shifted(values, edge, ahead):
    line = lax.broadcasted_iota(jnp.int32, values.shape, 0)
    if ahead:
        return jnp.where(line == SPAN - 1, edge, pltpu.roll(values, SPAN - 1, axis=0))
    return jnp.where(line == 0, edge, pltpu.roll(values, 1, axis=0))


def clip_scalars(lengths, first, count):
    found = [jnp.int32(0)] * count
    start = jnp.int32(0)
    for k in range(lengths.shape[0]):
        for n in range(count):
            t = first + n
            found[n] = jnp.where(start <= t, t - start, found[n])
        start = start + lengths[k]
    return found


def spread_latents(all_ref, q_ref, distance, sx, top, bottom):
    depth = SOURCES * 2 * 128
    index = lax.broadcasted_iota(jnp.int32, (depth, 1), 0)
    source = index // 256
    side = (index // 128) % 2
    half = (index // 64) % 2
    frame = (index // 32) % 2
    x = index % 32
    column = jnp.where(side == sx, x, jnp.where(sx == 0, x + COLS, x - COLS))
    wanted = (column >= -HALO) & (column < COLS + HALO)
    target = (2 * source + frame) * WIDE + column + LEAD + 1
    lane = lax.broadcasted_iota(jnp.int32, (depth, 384), 1)
    spread = []
    for h in range(2):
        to = jnp.where(wanted & (half == h), target, -1)
        pick = jnp.where(lane == to, 1.0, 0.0).astype(BF)
        bands = (0, 16 + HALO) if h else (HALO, BAND)
        rows = (bands[1] - bands[0]) * 16
        lhs = jnp.concatenate(
            [
                all_ref[t, s, bands[0] : bands[1]].reshape(rows, 128)
                for t in range(SOURCES)
                for s in range(2)
            ],
            axis=1,
        )
        spread.append(jnp.dot(lhs, pick, preferred_element_type=F32))
    lower, upper = spread
    edge = HALO * 16
    pt = jnp.concatenate(
        [
            upper[:edge] * top.astype(F32),
            lower[: 16 * 16],
            upper[edge:],
            lower[16 * 16 :] * bottom.astype(F32),
        ],
        axis=0,
    )
    pt = pt.astype(BF)
    cell = lax.broadcasted_iota(jnp.int32, (1, CELLS), 1)
    beyond = cell - INNER
    halo = beyond // 6
    frame_of = jnp.where(cell < INNER, cell // 32, beyond - 6 * halo)
    column = jnp.where(
        cell < INNER,
        2 * (cell % SPAN) + (cell // SPAN) % 2,
        jnp.where(halo < 2, halo - 2, COLS + halo - 2),
    )
    base = frame_of * WIDE + column + LEAD
    line = lax.broadcasted_iota(jnp.int32, (384, CELLS), 0)
    for lag in range(3):
        keep = jnp.zeros((1, CELLS), jnp.int32)
        for f in range(6):
            keep = jnp.where(frame_of == f, (distance[f] >= lag).astype(jnp.int32), keep)
        keep = jnp.where(cell < USED, keep, 0)
        for dx in range(3):
            to = jnp.where(keep == 1, base + (2 - lag) * WIDE + dx, -1)
            pick = jnp.where(line == to, 1.0, 0.0).astype(BF)
            q_ref[3 * lag + dx] = jnp.dot(pt, pick, preferred_element_type=F32).astype(BF)


def main_kernel(
    lengths, all_ref, we_ref, g1_ref, g2_ref, w1_hbm, w2_hbm, u1_hbm,
    out_ref, u2_hbm,
    q_ref, f_ref, h_ref, s0_ref, s1_ref, s2_ref, s3_ref, e_ref, xa_ref, xb_ref, hxa_ref, hxb_ref, ma_ref, mb_ref, acc_ref,
    w_ref, a_ref, b_ref, hn_ref, keep_ref, raw_ref, made_ref, sem, raw_sem, made_sem,
):
    tm = lax.axis_index("tm")
    sy = lax.axis_index("sy")
    sx = lax.axis_index("sx")
    top = (sy > 0).astype(jnp.int32)
    bottom = (sy < lax.axis_size("sy") - 1).astype(jnp.int32)
    left = sx == 0
    distance = clip_scalars(lengths, 2 * tm - 4, 6)
    s_refs = (s0_ref, s1_ref, s2_ref, s3_ref)
    x_refs, hx_refs, m_refs = (xa_ref, xb_ref), (hxa_ref, hxb_ref), (ma_ref, mb_ref)

    def pair_of(step):
        n = (0, 1, 1)[step // 4]
        whole = distance[3 + 2 * n] >= 1
        return (
            (distance[2 + 2 * n] >= 2).astype(F32),
            (distance[2 + 2 * n] >= 1).astype(F32),
            whole.astype(F32),
            whole,
        )

    def weight_copies(step):
        slot, tau = step % 2, step % 4
        w_hbm, u_hbm = (w1_hbm, u1_hbm) if step < 8 else (w2_hbm, u2_hbm)
        whole = pair_of(step)[3]
        which = (0, jnp.where(whole, 1, 4), jnp.where(whole, 2, 3), 3)[tau]
        mixed = pltpu.make_async_copy(
            u_hbm.at[pl.ds(2 * which, 2)], w_ref.at[slot, pl.ds(1, 2)], sem.at[slot, 0]
        )

        def outer(source, n):
            return pltpu.make_async_copy(source, w_ref.at[slot, 3 * n], sem.at[slot, 1 + n])

        tap = (0, 1, 2, 2)[tau]
        plain = [outer(w_hbm.at[tap, 2 * n], n) for n in range(2)]
        made = None
        if tau in (1, 2):
            made = [outer(u_hbm.at[8 + 2 * tau + n], n) for n in range(2)]
        return whole, mixed, plain, made

    def fetch(step):
        whole, mixed, plain, made = weight_copies(step)
        mixed.start()
        if made is None:
            for one in plain:
                one.start()
            return

        @pl.when(whole)
        def _():
            for one in made:
                one.start()

        @pl.when(jnp.logical_not(whole))
        def _():
            for one in plain:
                one.start()

    def arrive(step):
        _, mixed, plain, _ = weight_copies(step)
        mixed.wait()
        for one in plain:
            one.wait()

    def raw_copy(piece, slot):
        part = pl.ds(pl.multiple_of(piece * PIECE, PIECE), PIECE)
        return pltpu.make_async_copy(w2_hbm.at[:, :, part], raw_ref.at[slot], raw_sem.at[slot])

    def made_copy(piece, slot):
        part = pl.ds(pl.multiple_of(piece * PIECE, PIECE), PIECE)
        return pltpu.make_async_copy(made_ref.at[slot], u2_hbm.at[:, part], made_sem.at[slot])

    def piece_in(step, k):
        piece = QUARTERS * step + k
        raw_copy(piece, k).wait()
        if step > 0:
            made_copy(piece - QUARTERS, k).wait()
        if step < PIECES // QUARTERS - 1:
            raw_copy(piece + AHEAD, lax.rem(k + AHEAD, QUARTERS)).start()
        else:

            @pl.when(k + AHEAD < QUARTERS)
            def _():
                raw_copy(piece + AHEAD, lax.rem(k + AHEAD, QUARTERS)).start()

    def piece_made(step, k):
        slot = k
        for block in range(PIECE // 16):
            rows = slice(block * 16, (block + 1) * 16)
            for lane in range(3):
                lanes = slice(lane * 128, (lane + 1) * 128)
                w = [
                    [raw_ref[slot, t, y, rows, lanes].astype(F32) for y in range(3)]
                    for t in range(3)
                ]

                def put(n, value, rows=rows, lanes=lanes):
                    made_ref[slot, n, rows, lanes] = value.astype(BF)

                mix_weights(w, put)

    def piece_out(step, k):
        made_copy(QUARTERS * step + k, k).start()

    fetch(0)
    for k in range(AHEAD):
        raw_copy(k, k).start()
    spread_latents(all_ref, q_ref, distance, sx, top, bottom)
    cell = lax.broadcasted_iota(jnp.int32, (USED, 128), 0)
    off_left = (cell >= INNER) & (cell < INNER + 12)
    off_right = cell >= INNER + 12
    keep_ref[...] = jnp.where((off_left & left) | (off_right & (sx == 1)), 0.0, 1.0)
    first_gain = g1_ref[...][None, :] * 0.5
    second_gain = g2_ref[...][None, :] * 0.5
    h_ref[...] = jnp.zeros_like(h_ref)

    @pl.loop(0, R1 // ENTRY_ROWS)
    def _(block):
        cols = []
        for n in range(ENTRY_ROWS):
            first = pl.multiple_of((block * ENTRY_ROWS + n) * 16, 16)
            cols.append(
                jnp.concatenate(
                    [
                        q_ref[3 * lag + dx, pl.ds(first + 16 * dy, 16), :]
                        for lag in (2, 1, 0)
                        for dy in range(3)
                        for dx in range(3)
                    ],
                    axis=0,
                )
            )
        patches = jnp.concatenate(cols, axis=1)
        entry = lax.dot_general(
            patches, we_ref[...], (((0,), (0,)), ((), ())), preferred_element_type=F32
        ).astype(BF)
        for n in range(ENTRY_ROWS):
            row = block * ENTRY_ROWS + n
            inside = jnp.where(row < 2, top, jnp.where(row >= R1 - 2, bottom, 1)).astype(F32)
            value = entry[n * CELLS : n * CELLS + USED].astype(F32)
            for f in range(2):
                e_ref[f, row] = entry[n * CELLS + (4 + f) * 32 : n * CELLS + (5 + f) * 32]
            a_ref[n] = norm_act_wide(value, first_gain, keep_ref[...] * inside)
        for n in range(ENTRY_ROWS):
            row = block * ENTRY_ROWS + n
            for f in range(6):
                even = a_ref[n, f * 32 : f * 32 + SPAN, :]
                odd = a_ref[n, f * 32 + SPAN : f * 32 + 2 * SPAN, :]
                before = a_ref[n, INNER + 6 + f : INNER + 7 + f, :]
                after = a_ref[n, INNER + 12 + f : INNER + 13 + f, :]
                f_ref[f, row, 0] = shifted(odd, before, False).astype(BF)
                f_ref[f, row, 1] = even.astype(BF)
                f_ref[f, row, 2] = odd.astype(BF)
                f_ref[f, row, 3] = shifted(even, after, True).astype(BF)
                places = (
                    jnp.where(left, f * 32 + 31, INNER + f),
                    jnp.where(left, INNER + 12 + f, INNER + 6 + f),
                    jnp.where(left, INNER + 18 + f, f * 32),
                )
                for dx, place in enumerate(places):
                    h_ref[f, n % 2, pl.ds(row // 2, 1), dx * C : (dx + 1) * C] = a_ref[
                        n, pl.ds(place, 1), :
                    ]

    def time_mix(step, one, dtype):
        tau = step % 4
        k0, k1, s, _ = pair_of(step)
        base = 2 if 4 <= step < 8 else 0

        def scaled(value, by):
            if dtype == F32:
                return value * by
            tile = jnp.full((16, 128), by, F32).astype(BF)
            return value * jnp.tile(tile, (1, value.shape[1] // 128))

        if tau == 0:
            return scaled(one(base), k0) - scaled(one(base + 2), s)
        if tau == 1:
            return scaled(one(base + 1), k1) + scaled(one(base + 2), s)
        if tau == 2:
            return one(base + 2) - scaled(one(base + 1), s * k1)
        return scaled(one(base + 1), s * k1) - one(base + 3)

    def row_transform(d):
        return d[0] - d[2], d[1] + d[2], d[2] - d[1], d[1] - d[3]

    def build(step, i):
        def read(frame, row, j):
            return f_ref[frame, row, j] if step < 8 else s_refs[frame][row, j]

        x_ref = x_refs[step % 2]
        for j in range(4):
            d = [
                time_mix(step, lambda frame, k=k: read(frame, 2 * i + k, j), BF)
                for k in range(4)
            ]
            for k, value in enumerate(row_transform(d)):
                x_ref[k, j, pl.ds(pl.multiple_of(i * SPAN, SPAN), SPAN), :] = value

    def build_halo(step):
        hx_ref = hx_refs[step % 2]
        for dx in range(3):
            lanes = slice(dx * C, (dx + 1) * C)
            d = [
                time_mix(
                    step,
                    lambda frame, k=k: h_ref[frame, k % 2, pl.ds(k // 2, HALO_ROWS), lanes],
                    F32,
                )
                for k in range(4)
            ]
            for k, value in enumerate(row_transform(d)):
                hx_ref[k, :, lanes] = value.astype(BF)

    def settle(step, part):
        tau = step % 4
        m_ref = m_refs[step % 2]
        s = pair_of(step)[2]
        t = [m_ref[k, part, :] for k in range(4)]
        middle = t[1] - t[2]
        both = (t[0] + t[1] + t[2], middle - t[3])
        if tau == 3:
            return 1, [acc_ref[1, p, part, :] - both[p] for p in range(2)]
        if tau == 2:
            for p in range(2):
                acc_ref[1, p, part, :] = acc_ref[1, p, part, :] - s * both[p]
            return 0, [acc_ref[0, p, part, :] + both[p] for p in range(2)]
        for p in range(2):
            if tau == 0:
                acc_ref[0, p, part, :] = both[p]
            else:
                acc_ref[0, p, part, :] = acc_ref[0, p, part, :] + both[p]
                acc_ref[1, p, part, :] = s * both[p]
        return None

    def settle_halo(step):
        done = settle(step, pl.ds(2 * I1 * SPAN, HALO_ROWS))
        if done is not None:
            for p, value in enumerate(done[1]):
                hn_ref[p] = norm_act(value, second_gain, 1.0)

    def settle_first(step, i):
        for side in range(2):
            first = pl.multiple_of(side * I1 * SPAN + i * SPAN, SPAN)
            done = settle(step, pl.ds(first, SPAN))
            if done is None:
                continue
            frame = 2 * (step // 4) + done[0]
            for p, value in enumerate(done[1]):
                row = 2 * i + p
                inside = jnp.where(row == 0, top, jnp.where(row == R2 - 1, bottom, 1)).astype(F32)
                value = norm_act(value, second_gain, inside)
                here = inside * jnp.where(sx == side, 1.0, 0.0)
                edge = hn_ref[p, pl.ds(i, 1), :] * here
                if side == 0:
                    s_refs[frame][row, 1] = value.astype(BF)
                    s_refs[frame][row, 3] = shifted(value, edge, True).astype(BF)
                else:
                    s_refs[frame][row, 2] = value.astype(BF)
                    s_refs[frame][row, 0] = shifted(value, edge, False).astype(BF)

    def settle_second(step, i, n):
        done = [
            settle(step, pl.ds(pl.multiple_of(side * I2 * SPAN + i * SPAN, SPAN), SPAN))
            for side in range(2)
        ]
        if done[0] is None:
            return
        member = done[0][0]
        for p in range(2):
            row = 2 * i + p
            for side in range(2):
                part = slice(side * SPAN, (side + 1) * SPAN)
                value = done[side][1][p] + e_ref[member, row + 2, part, :].astype(F32)
                for lane in range(3):
                    b_ref[2 * n + p, lane, pl.ds(side, SPAN, stride=2), :] = value[
                        :, lane * 128 : (lane + 1) * 128
                    ]
            for lane in range(3):
                out_ref[member, row, :, lane * 128 : (lane + 1) * 128] = b_ref[
                    2 * n + p, lane
                ].astype(BF)

    def products(step, k):
        x_ref, m_ref = x_refs[step % 2], m_refs[step % 2]
        count = (I1 if step < 8 else I2) * SPAN
        x = [x_ref[k, j, :count, :] for j in range(4)]
        parts = [jnp.concatenate(x[:3], axis=1), jnp.concatenate(x[1:], axis=1)]
        if step < 8:
            parts.append(hx_refs[step % 2][k])
        lhs = jnp.concatenate(parts, axis=0)
        m_ref[k, : lhs.shape[0], :] = jnp.dot(
            lhs, w_ref[step % 2, k], preferred_element_type=F32
        )

    def build_alone(step):
        @pl.loop(0, I1 if step < 8 else I2)
        def _(i):
            build(step, i)

        if step < 8:
            build_halo(step)

    def run(step):
        arrive(step)
        if step < 11:
            fetch(step + 1)
        builds = step < 11
        settles = step > 0
        pieces = step < PIECES // QUARTERS
        if builds and step < 7:
            build(step + 1, I1 - 1)
            build_halo(step + 1)
        if settles and step < 9:
            settle_halo(step - 1)
            settle_first(step - 1, I1 - 1)

        @pl.loop(0, QUARTERS)
        def _(k):
            if pieces:
                piece_in(step, k)
            products(step, k)
            for n in range(QUARTER if settles else 0):
                if step < 9:
                    settle_first(step - 1, QUARTER * k + n)
                else:
                    settle_second(step - 1, QUARTER * k + n, n)
            for n in range(QUARTER if builds else 0):
                i = QUARTER * k + n
                build(step + 1, jnp.maximum(i - 1, 0) if step == 7 else i)
            if pieces:
                piece_made(step, k)
                piece_out(step, k)

        if step == PIECES // QUARTERS - 1:
            for k in range(QUARTERS):
                made_copy(QUARTERS * step + k, k).wait()
        if step == 7:
            build(8, I2 - 1)

    @pl.loop(0, I1)
    def _(i):
        build(0, i)

    build_halo(0)
    for step in range(12):
        run(step)

    @pl.loop(0, QUARTERS)
    def _(k):
        for n in range(QUARTER):
            settle_second(11, QUARTER * k + n, n)


def block_call(*operands):
    vmem = pl.BlockSpec(memory_space=pltpu.VMEM)
    smem = pl.BlockSpec(memory_space=pltpu.SMEM)
    hbm = pl.BlockSpec(memory_space=pl.ANY)
    m1 = 2 * I1 * SPAN + HALO_ROWS
    return pl.pallas_call(
        main_kernel,
        in_specs=[smem, vmem, vmem, vmem, vmem, hbm, hbm, hbm],
        out_specs=[vmem, hbm],
        out_shape=[
            jax.ShapeDtypeStruct((2, ROWS, COLS, C), BF),
            jax.ShapeDtypeStruct((SETS, K3, C), BF),
        ],
        scratch_shapes=[
            pltpu.VMEM((9, 38 * 16, CELLS), BF),
            pltpu.VMEM((6, R1, 4, SPAN, C), BF),
            pltpu.VMEM((6, 2, HALO_ROWS + 8, K3), F32),
            pltpu.VMEM((R2, 4, SPAN, C), BF),
            pltpu.VMEM((R2, 4, SPAN, C), BF),
            pltpu.VMEM((R2, 4, SPAN, C), BF),
            pltpu.VMEM((R2, 4, SPAN, C), BF),
            pltpu.VMEM((2, R1, COLS, C), BF),
            pltpu.VMEM((4, 4, I1 * SPAN, C), BF),
            pltpu.VMEM((4, 4, I1 * SPAN, C), BF),
            pltpu.VMEM((4, HALO_ROWS, K3), BF),
            pltpu.VMEM((4, HALO_ROWS, K3), BF),
            pltpu.VMEM((4, m1, C), F32),
            pltpu.VMEM((4, m1, C), F32),
            pltpu.VMEM((2, 2, m1, C), F32),
            pltpu.VMEM((2, 4, K3, C), BF),
            pltpu.VMEM((ENTRY_ROWS, USED, C), F32),
            pltpu.VMEM((2 * QUARTER, 3, COLS, 128), F32),
            pltpu.VMEM((2, HALO_ROWS, C), F32),
            pltpu.VMEM((USED, 128), F32),
            pltpu.VMEM((QUARTERS, 3, 3, PIECE, C), BF),
            pltpu.VMEM((QUARTERS, SETS, PIECE, C), BF),
            pltpu.SemaphoreType.DMA((2, 3)),
            pltpu.SemaphoreType.DMA((QUARTERS,)),
            pltpu.SemaphoreType.DMA((QUARTERS,)),
        ],
        compiler_params=pltpu.CompilerParams(vmem_limit_bytes=62 * MIB),
        name="block",
    )(*operands)[0]


def body(latent, clip_lengths, entry_kernel, first_gain, first_kernel, second_gain, second_kernel):
    own = latent.reshape(2, 2, 16, COLS, 16).transpose(2, 4, 1, 0, 3).reshape(16, 16, 128)
    everything, u1 = gathered(own, first_kernel)
    return block_call(
        clip_lengths,
        everything,
        entry_kernel.reshape(27 * 16, C),
        first_gain,
        second_gain,
        first_kernel.reshape(3, 3, K3, C),
        second_kernel.reshape(3, 3, K3, C),
        u1.reshape(SETS, K3, C),
    )


def solution(mesh):
    return jax.shard_map(
        body,
        mesh=mesh,
        in_specs=(P("tm", "sy", "sx", None), P(), P(), P(), P(), P(), P()),
        out_specs=P("tm", "sy", "sx", None),
        check_vma=False,
    )
```

```python
import functools

import jax
import jax.numpy as jnp
from jax import lax
from jax.experimental import pallas as pl
from jax.experimental.pallas import tpu as pltpu
from jax.sharding import PartitionSpec as P

C = 384
K3 = 3 * C
MIB = 2**20
BF = jnp.bfloat16
F32 = jnp.float32


MESH = pl.DeviceIdType.MESH
ROWS = 32
COLS = 32
HALO = 3
BAND = 16 + 2 * HALO
SOURCES = 4
WEIGHT_STEPS = 9
LAST = WEIGHT_STEPS - 1
PARTNERS = [(k, d) for k in range(SOURCES) for d in (0, 1, -1) if (k, d) != (0, 0)]
SENT = {0: (0, 16), 1: (16 - HALO, HALO), -1: (0, HALO)}
LANDS = {0: HALO, 1: 0, -1: HALO + 16}
SETS = 14
ENTERED = 1
LANDED = 6


def mix_weights(w, put):
    edge = [w[0][y] + w[2][y] for y in range(3)]
    times = [
        w[0],
        [(edge[y] + w[1][y]) * 0.5 for y in range(3)],
        [(edge[y] - w[1][y]) * 0.5 for y in range(3)],
        w[2],
        w[1],
    ]
    for t, g in enumerate(times):
        outer = g[0] + g[2]
        put(2 * t, (outer + g[1]) * 0.5)
        put(2 * t + 1, (outer - g[1]) * 0.5)
    for n, t in enumerate((1, 2)):
        put(10 + 2 * n, times[t][0])
        put(11 + 2 * n, times[t][2])


def weight_block(w_ref, u_ref):
    step = 16

    @pl.loop(0, w_ref.shape[3] // step)
    def _(block):
        part = pl.ds(pl.multiple_of(block * step, step), step)
        for lane in range(3):
            lanes = slice(lane * 128, (lane + 1) * 128)
            w = [[w_ref[t, y, 0, part, lanes].astype(F32) for y in range(3)] for t in range(3)]

            def put(n, value, lanes=lanes):
                u_ref[n, 0, part, lanes] = value.astype(BF)

            mix_weights(w, put)


def gather_kernel(
    latent_ref, w1_ref, all_ref, u1_ref, own_ref, send_sem, recv_sem, local_sem, pair_sem
):
    step = pl.program_id(0)
    tm = lax.axis_index("tm")
    sy = lax.axis_index("sy")
    sx = lax.axis_index("sx")
    tms = lax.axis_size("tm")
    sys = lax.axis_size("sy")

    def place(k, d):
        return (lax.rem(tm + k + tms, tms), lax.rem(sy + d + sys, sys), sx)

    def copy(n):
        k, d = PARTNERS[n]
        first, count = SENT[d]
        return pltpu.make_async_remote_copy(
            src_ref=own_ref.at[pl.ds(first, count)],
            dst_ref=all_ref.at[SOURCES - 1 - k, sx, pl.ds(LANDS[d], count)],
            send_sem=send_sem.at[n],
            recv_sem=recv_sem.at[n],
            device_id=place(k, d),
            device_id_type=MESH,
        )

    def local():
        return pltpu.make_async_copy(
            own_ref, all_ref.at[SOURCES - 1, sx, pl.ds(HALO, 16)], local_sem
        )

    def across():
        return pltpu.make_async_remote_copy(
            src_ref=all_ref.at[:, sx],
            dst_ref=all_ref.at[:, sx],
            send_sem=pair_sem.at[0],
            recv_sem=pair_sem.at[1],
            device_id=(tm, sy, 1 - sx),
            device_id_type=MESH,
        )

    @pl.when(step == 0)
    def _():
        barrier = pltpu.get_barrier_semaphore()
        for k, d in PARTNERS:
            pl.semaphore_signal(barrier, inc=1, device_id=place(-k, -d), device_id_type=MESH)
        pl.semaphore_signal(barrier, inc=1, device_id=(tm, sy, 1 - sx), device_id_type=MESH)
        line = lax.broadcasted_iota(jnp.int32, (COLS, 128), 0)
        lane = lax.broadcasted_iota(jnp.int32, (COLS, 128), 1)
        packed = jnp.zeros((16 * 16, 128), F32)
        for half in range(2):
            for f in range(2):
                to = jnp.where(lane == line + (2 * half + f) * COLS, 1.0, 0.0).astype(BF)
                rows = latent_ref[f, half * 16 : (half + 1) * 16].reshape(16 * 16, COLS)
                packed = packed + jnp.dot(rows, to, preferred_element_type=F32)
        own_ref[...] = packed.astype(BF).reshape(16, 16, 128)
        local().start()

    @pl.when(step == ENTERED)
    def _():
        pl.semaphore_wait(pltpu.get_barrier_semaphore(), len(PARTNERS) + 1)
        for n in range(len(PARTNERS)):
            copy(n).start()

    weight_block(w1_ref, u1_ref)

    @pl.when(step == LANDED)
    def _():
        local().wait()
        for n in range(len(PARTNERS)):
            copy(n).wait()
        across().start()

    @pl.when(step == LAST)
    def _():
        across().wait()


def gathered(latent, first_kernel):
    chunk = C // 3
    hbm = pl.BlockSpec(memory_space=pl.ANY)
    copies = len(PARTNERS)
    return pl.pallas_call(
        gather_kernel,
        grid=(WEIGHT_STEPS,),
        in_specs=[
            pl.BlockSpec(memory_space=pltpu.VMEM),
            pl.BlockSpec((3, 3, 1, chunk, C), lambda step: (0, 0, step // 3, step % 3, 0)),
        ],
        out_specs=[
            hbm,
            pl.BlockSpec((SETS, 1, chunk, C), lambda step: (0, step // 3, step % 3, 0)),
        ],
        out_shape=[
            jax.ShapeDtypeStruct((SOURCES, 2, BAND, 16, 128), BF),
            jax.ShapeDtypeStruct((SETS, 3, C, C), BF),
        ],
        scratch_shapes=[
            pltpu.VMEM((16, 16, 128), BF),
            pltpu.SemaphoreType.DMA((copies,)),
            pltpu.SemaphoreType.DMA((copies,)),
            pltpu.SemaphoreType.DMA,
            pltpu.SemaphoreType.DMA((2,)),
        ],
        compiler_params=pltpu.CompilerParams(
            vmem_limit_bytes=62 * MIB, collective_id=0, has_side_effects=True
        ),
        cost_estimate=pl.CostEstimate(
            flops=60 * 9 * C * C, bytes_accessed=41 * 3 * C * C * 2, transcendentals=0
        ),
        name="gather",
    )(latent, first_kernel)


WIDE = 40
LEAD = 9
SPAN = 16
CELLS = 256
USED = 6 * 2 * SPAN + 24
INNER = 6 * 2 * SPAN
R1 = ROWS + 4
R2 = ROWS + 2
I1 = R2 // 2
I2 = ROWS // 2
HALO_ROWS = 32
ENTRY_ROWS = 12
QUARTER = 4
QUARTERS = 4
PIECE = 48
PIECES = K3 // PIECE
AHEAD = 3


def norm_act(values, gain, keep):
    mean = jnp.mean(values * values, axis=-1, keepdims=True)
    half = values * (lax.rsqrt(mean + 1e-6) * keep) * gain
    return half * jnp.tanh(half) + half


def norm_act_wide(values, gain, keep):
    squares = values * values
    folded = squares[:, :128] + squares[:, 128:256] + squares[:, 256:]
    ones = jnp.full((128, 128), 1.0, BF)
    mean = jnp.dot(folded.astype(BF), ones, preferred_element_type=F32) * (1.0 / C)
    scale = lax.rsqrt(mean + 1e-6) * keep
    half = values * jnp.concatenate([scale] * 3, axis=1) * gain
    return half * jnp.tanh(half) + half


def shifted(values, edge, ahead):
    line = lax.broadcasted_iota(jnp.int32, values.shape, 0)
    if ahead:
        return jnp.where(line == SPAN - 1, edge, pltpu.roll(values, SPAN - 1, axis=0))
    return jnp.where(line == 0, edge, pltpu.roll(values, 1, axis=0))


def clip_scalars(lengths, first, count):
    found = [jnp.int32(0)] * count
    start = jnp.int32(0)
    for k in range(lengths.shape[0]):
        for n in range(count):
            t = first + n
            found[n] = jnp.where(start <= t, t - start, found[n])
        start = start + lengths[k]
    return found


def spread_latents(all_ref, q_ref, distance, sx, top, bottom):
    depth = SOURCES * 2 * 128
    index = lax.broadcasted_iota(jnp.int32, (depth, 1), 0)
    source = index // 256
    side = (index // 128) % 2
    half = (index // 64) % 2
    frame = (index // 32) % 2
    x = index % 32
    column = jnp.where(side == sx, x, jnp.where(sx == 0, x + COLS, x - COLS))
    wanted = (column >= -HALO) & (column < COLS + HALO)
    target = (2 * source + frame) * WIDE + column + LEAD + 1
    lane = lax.broadcasted_iota(jnp.int32, (depth, 384), 1)
    spread = []
    for h in range(2):
        to = jnp.where(wanted & (half == h), target, -1)
        pick = jnp.where(lane == to, 1.0, 0.0).astype(BF)
        bands = (0, 16 + HALO) if h else (HALO, BAND)
        rows = (bands[1] - bands[0]) * 16
        lhs = jnp.concatenate(
            [
                all_ref[t, s, bands[0] : bands[1]].reshape(rows, 128)
                for t in range(SOURCES)
                for s in range(2)
            ],
            axis=1,
        )
        spread.append(jnp.dot(lhs, pick, preferred_element_type=F32))
    lower, upper = spread
    edge = HALO * 16
    pt = jnp.concatenate(
        [
            upper[:edge] * top.astype(F32),
            lower[: 16 * 16],
            upper[edge:],
            lower[16 * 16 :] * bottom.astype(F32),
        ],
        axis=0,
    )
    pt = pt.astype(BF)
    cell = lax.broadcasted_iota(jnp.int32, (1, CELLS), 1)
    beyond = cell - INNER
    halo = beyond // 6
    frame_of = jnp.where(cell < INNER, cell // 32, beyond - 6 * halo)
    column = jnp.where(
        cell < INNER,
        2 * (cell % SPAN) + (cell // SPAN) % 2,
        jnp.where(halo < 2, halo - 2, COLS + halo - 2),
    )
    base = frame_of * WIDE + column + LEAD
    line = lax.broadcasted_iota(jnp.int32, (384, CELLS), 0)
    for lag in range(3):
        keep = jnp.zeros((1, CELLS), jnp.int32)
        for f in range(6):
            keep = jnp.where(frame_of == f, (distance[f] >= lag).astype(jnp.int32), keep)
        keep = jnp.where(cell < USED, keep, 0)
        for dx in range(3):
            to = jnp.where(keep == 1, base + (2 - lag) * WIDE + dx, -1)
            pick = jnp.where(line == to, 1.0, 0.0).astype(BF)
            q_ref[3 * lag + dx] = jnp.dot(pt, pick, preferred_element_type=F32).astype(BF)


def main_kernel(
    lengths, all_ref, we_ref, g1_ref, g2_ref, w1_hbm, w2_hbm, u1_hbm,
    out_hbm, u2_hbm,
    q_ref, f_ref, h_ref, s0_ref, s1_ref, s2_ref, s3_ref, e_ref, xa_ref, xb_ref, hxa_ref, hxb_ref, ma_ref, mb_ref, acc_ref,
    w_ref, a_ref, b_ref, hn_ref, keep_ref, raw_ref, made_ref, out_ref, sem, raw_sem, made_sem,
    out_sem,
):
    tm = lax.axis_index("tm")
    sy = lax.axis_index("sy")
    sx = lax.axis_index("sx")
    top = (sy > 0).astype(jnp.int32)
    bottom = (sy < lax.axis_size("sy") - 1).astype(jnp.int32)
    left = sx == 0
    distance = clip_scalars(lengths, 2 * tm - 4, 6)
    s_refs = (s0_ref, s1_ref, s2_ref, s3_ref)
    x_refs, hx_refs, m_refs = (xa_ref, xb_ref), (hxa_ref, hxb_ref), (ma_ref, mb_ref)

    def pair_of(step):
        n = (0, 1, 1)[step // 4]
        whole = distance[3 + 2 * n] >= 1
        return (
            (distance[2 + 2 * n] >= 2).astype(F32),
            (distance[2 + 2 * n] >= 1).astype(F32),
            whole.astype(F32),
            whole,
        )

    def weight_copies(step):
        slot, tau = step % 2, step % 4
        w_hbm, u_hbm = (w1_hbm, u1_hbm) if step < 8 else (w2_hbm, u2_hbm)
        whole = pair_of(step)[3]
        which = (0, jnp.where(whole, 1, 4), jnp.where(whole, 2, 3), 3)[tau]
        mixed = pltpu.make_async_copy(
            u_hbm.at[pl.ds(2 * which, 2)], w_ref.at[slot, pl.ds(1, 2)], sem.at[slot, 0]
        )

        def outer(source, n):
            return pltpu.make_async_copy(source, w_ref.at[slot, 3 * n], sem.at[slot, 1 + n])

        tap = (0, 1, 2, 2)[tau]
        plain = [outer(w_hbm.at[tap, 2 * n], n) for n in range(2)]
        made = None
        if tau in (1, 2):
            made = [outer(u_hbm.at[8 + 2 * tau + n], n) for n in range(2)]
        return whole, mixed, plain, made

    def fetch(step):
        whole, mixed, plain, made = weight_copies(step)
        mixed.start()
        if made is None:
            for one in plain:
                one.start()
            return

        @pl.when(whole)
        def _():
            for one in made:
                one.start()

        @pl.when(jnp.logical_not(whole))
        def _():
            for one in plain:
                one.start()

    def arrive(step):
        _, mixed, plain, _ = weight_copies(step)
        mixed.wait()
        for one in plain:
            one.wait()

    def raw_copy(piece, slot):
        part = pl.ds(pl.multiple_of(piece * PIECE, PIECE), PIECE)
        return pltpu.make_async_copy(w2_hbm.at[:, :, part], raw_ref.at[slot], raw_sem.at[slot])

    def made_copy(piece, slot):
        part = pl.ds(pl.multiple_of(piece * PIECE, PIECE), PIECE)
        return pltpu.make_async_copy(made_ref.at[slot], u2_hbm.at[:, part], made_sem.at[slot])

    def piece_in(step, k):
        piece = QUARTERS * step + k
        raw_copy(piece, k).wait()
        if step > 0:
            made_copy(piece - QUARTERS, k).wait()
        if step < PIECES // QUARTERS - 1:
            raw_copy(piece + AHEAD, lax.rem(k + AHEAD, QUARTERS)).start()
        else:

            @pl.when(k + AHEAD < QUARTERS)
            def _():
                raw_copy(piece + AHEAD, lax.rem(k + AHEAD, QUARTERS)).start()

    def piece_made(step, k):
        slot = k
        for block in range(PIECE // 16):
            rows = slice(block * 16, (block + 1) * 16)
            for lane in range(3):
                lanes = slice(lane * 128, (lane + 1) * 128)
                w = [
                    [raw_ref[slot, t, y, rows, lanes] for y in range(3)]
                    for t in range(3)
                ]

                def put(n, value, rows=rows, lanes=lanes):
                    made_ref[slot, n, rows, lanes] = value

                mix_weights(w, put)

    def piece_out(step, k):
        made_copy(QUARTERS * step + k, k).start()

    fetch(0)
    for k in range(AHEAD):
        raw_copy(k, k).start()
    spread_latents(all_ref, q_ref, distance, sx, top, bottom)
    cell = lax.broadcasted_iota(jnp.int32, (USED, 128), 0)
    off_left = (cell >= INNER) & (cell < INNER + 12)
    off_right = cell >= INNER + 12
    keep_ref[...] = jnp.where((off_left & left) | (off_right & (sx == 1)), 0.0, 1.0)
    first_gain = g1_ref[...][None, :] * 0.5
    second_gain = g2_ref[...][None, :] * 0.5
    h_ref[...] = jnp.zeros_like(h_ref)

    @pl.loop(0, R1 // ENTRY_ROWS)
    def _(block):
        cols = []
        for n in range(ENTRY_ROWS):
            first = pl.multiple_of((block * ENTRY_ROWS + n) * 16, 16)
            cols.append(
                jnp.concatenate(
                    [
                        q_ref[3 * lag + dx, pl.ds(first + 16 * dy, 16), :]
                        for lag in (2, 1, 0)
                        for dy in range(3)
                        for dx in range(3)
                    ],
                    axis=0,
                )
            )
        patches = jnp.concatenate(cols, axis=1)
        entry = lax.dot_general(
            patches, we_ref[...], (((0,), (0,)), ((), ())), preferred_element_type=F32
        ).astype(BF)
        for n in range(ENTRY_ROWS):
            row = block * ENTRY_ROWS + n
            inside = jnp.where(row < 2, top, jnp.where(row >= R1 - 2, bottom, 1)).astype(F32)
            value = entry[n * CELLS : n * CELLS + USED].astype(F32)
            for f in range(2):
                e_ref[f, row] = entry[n * CELLS + (4 + f) * 32 : n * CELLS + (5 + f) * 32]
            a_ref[n] = norm_act_wide(value, first_gain, keep_ref[...] * inside)
        for n in range(ENTRY_ROWS):
            row = block * ENTRY_ROWS + n
            for f in range(6):
                even = a_ref[n, f * 32 : f * 32 + SPAN, :]
                odd = a_ref[n, f * 32 + SPAN : f * 32 + 2 * SPAN, :]
                before = a_ref[n, INNER + 6 + f : INNER + 7 + f, :]
                after = a_ref[n, INNER + 12 + f : INNER + 13 + f, :]
                f_ref[f, row, 0] = shifted(odd, before, False).astype(BF)
                f_ref[f, row, 1] = even.astype(BF)
                f_ref[f, row, 2] = odd.astype(BF)
                f_ref[f, row, 3] = shifted(even, after, True).astype(BF)
                places = (
                    jnp.where(left, f * 32 + 31, INNER + f),
                    jnp.where(left, INNER + 12 + f, INNER + 6 + f),
                    jnp.where(left, INNER + 18 + f, f * 32),
                )
                for dx, place in enumerate(places):
                    h_ref[f, n % 2, pl.ds(row // 2, 1), dx * C : (dx + 1) * C] = a_ref[
                        n, pl.ds(place, 1), :
                    ]

    def time_mix(step, one, dtype):
        tau = step % 4
        k0, k1, s, _ = pair_of(step)
        base = 2 if 4 <= step < 8 else 0

        def scaled(value, by):
            if dtype == F32:
                return value * by
            tile = jnp.full((16, 128), by, F32).astype(BF)
            return value * jnp.tile(tile, (1, value.shape[1] // 128))

        if tau == 0:
            return scaled(one(base), k0) - scaled(one(base + 2), s)
        if tau == 1:
            return scaled(one(base + 1), k1) + scaled(one(base + 2), s)
        if tau == 2:
            return one(base + 2) - scaled(one(base + 1), s * k1)
        return scaled(one(base + 1), s * k1) - one(base + 3)

    def row_transform(d):
        return d[0] - d[2], d[1] + d[2], d[2] - d[1], d[1] - d[3]

    def build(step, i, count=1):
        def read(frame, row, j):
            return f_ref[frame, row, j] if step < 8 else s_refs[frame][row, j]

        x_ref = x_refs[step % 2]
        for j in range(4):
            d = [
                time_mix(step, lambda frame, k=k: read(frame, 2 * i + k, j), BF)
                for k in range(2 * count + 2)
            ]
            for n in range(count):
                part = pl.ds(pl.multiple_of((i + n) * SPAN, SPAN), SPAN)
                for k, value in enumerate(row_transform(d[2 * n : 2 * n + 4])):
                    x_ref[k, j, part, :] = value

    def build_halo(step):
        hx_ref = hx_refs[step % 2]
        for dx in range(3):
            lanes = slice(dx * C, (dx + 1) * C)
            d = [
                time_mix(
                    step,
                    lambda frame, k=k: h_ref[frame, k % 2, pl.ds(k // 2, HALO_ROWS), lanes],
                    F32,
                )
                for k in range(4)
            ]
            for k, value in enumerate(row_transform(d)):
                hx_ref[k, :, lanes] = value.astype(BF)

    def settle(step, part):
        tau = step % 4
        m_ref = m_refs[step % 2]
        s = pair_of(step)[2]
        t = [m_ref[k, part, :] for k in range(4)]
        middle = t[1] - t[2]
        both = (t[0] + t[1] + t[2], middle - t[3])
        if tau == 3:
            return 1, [acc_ref[1, p, part, :] - both[p] for p in range(2)]
        if tau == 2:
            for p in range(2):
                acc_ref[1, p, part, :] = acc_ref[1, p, part, :] - s * both[p]
            return 0, [acc_ref[0, p, part, :] + both[p] for p in range(2)]
        for p in range(2):
            if tau == 0:
                acc_ref[0, p, part, :] = both[p]
            else:
                acc_ref[0, p, part, :] = acc_ref[0, p, part, :] + both[p]
                acc_ref[1, p, part, :] = s * both[p]
        return None

    def settle_halo(step):
        done = settle(step, pl.ds(2 * I1 * SPAN, HALO_ROWS))
        if done is not None:
            for p, value in enumerate(done[1]):
                hn_ref[p] = norm_act(value, second_gain, 1.0)

    def settle_first(step, i):
        for side in range(2):
            first = pl.multiple_of(side * I1 * SPAN + i * SPAN, SPAN)
            done = settle(step, pl.ds(first, SPAN))
            if done is None:
                continue
            frame = 2 * (step // 4) + done[0]
            for p, value in enumerate(done[1]):
                row = 2 * i + p
                inside = jnp.where(row == 0, top, jnp.where(row == R2 - 1, bottom, 1)).astype(F32)
                value = norm_act(value, second_gain, inside)
                here = inside * jnp.where(sx == side, 1.0, 0.0)
                edge = hn_ref[p, pl.ds(i, 1), :] * here
                if side == 0:
                    s_refs[frame][row, 1] = value.astype(BF)
                    s_refs[frame][row, 3] = shifted(value, edge, True).astype(BF)
                else:
                    s_refs[frame][row, 2] = value.astype(BF)
                    s_refs[frame][row, 0] = shifted(value, edge, False).astype(BF)

    def settle_second(step, i, n):
        done = [
            settle(step, pl.ds(pl.multiple_of(side * I2 * SPAN + i * SPAN, SPAN), SPAN))
            for side in range(2)
        ]
        if done[0] is None:
            return
        member = done[0][0]
        for p in range(2):
            row = 2 * i + p
            for side in range(2):
                part = slice(side * SPAN, (side + 1) * SPAN)
                value = done[side][1][p] + e_ref[member, row + 2, part, :].astype(F32)
                for lane in range(3):
                    b_ref[2 * n + p, lane, pl.ds(side, SPAN, stride=2), :] = value[
                        :, lane * 128 : (lane + 1) * 128
                    ]
            for lane in range(3):
                out_ref[member, row, :, lane * 128 : (lane + 1) * 128] = b_ref[
                    2 * n + p, lane
                ].astype(BF)

    def products(step, k):
        x_ref, m_ref = x_refs[step % 2], m_refs[step % 2]
        count = (I1 if step < 8 else I2) * SPAN
        x = [x_ref[k, j, :count, :] for j in range(4)]
        parts = [jnp.concatenate(x[:3], axis=1), jnp.concatenate(x[1:], axis=1)]
        if step < 8:
            parts.append(hx_refs[step % 2][k])
        lhs = jnp.concatenate(parts, axis=0)
        m_ref[k, : lhs.shape[0], :] = jnp.dot(
            lhs, w_ref[step % 2, k], preferred_element_type=F32
        )

    def build_alone(step):
        @pl.loop(0, I1 if step < 8 else I2)
        def _(i):
            build(step, i)

        if step < 8:
            build_halo(step)

    def run(step):
        arrive(step)
        if step < 11:
            fetch(step + 1)
        builds = step < 11
        settles = step > 0
        pieces = step < PIECES // QUARTERS
        if builds and step < 7:
            build(step + 1, I1 - 1)
            build_halo(step + 1)
        if settles and step < 9:
            settle_halo(step - 1)
            settle_first(step - 1, I1 - 1)

        @pl.loop(0, QUARTERS)
        def _(k):
            if pieces:
                piece_in(step, k)
            products(step, k)
            for n in range(QUARTER if settles else 0):
                if step < 9:
                    settle_first(step - 1, QUARTER * k + n)
                else:
                    settle_second(step - 1, QUARTER * k + n, n)
            if step == 7:
                for n in range(QUARTER):
                    build(8, jnp.maximum(QUARTER * k + n - 1, 0))
            elif builds:
                build(step + 1, QUARTER * k, QUARTER)
            if pieces:
                piece_made(step, k)
                piece_out(step, k)

        if step == PIECES // QUARTERS - 1:
            for k in range(QUARTERS):
                made_copy(QUARTERS * step + k, k).wait()
        if step == 7:
            build(8, I2 - 1)

    @pl.loop(0, I1)
    def _(i):
        build(0, i)

    build_halo(0)
    for step in range(12):
        run(step)

    first_out = pltpu.make_async_copy(out_ref.at[0], out_hbm.at[0], out_sem.at[QUARTERS])
    first_out.start()

    def second_out(k):
        rows = pl.ds(2 * QUARTER * k, 2 * QUARTER)
        return pltpu.make_async_copy(out_ref.at[1, rows], out_hbm.at[1, rows], out_sem.at[k])

    @pl.loop(0, QUARTERS)
    def _(k):
        for n in range(QUARTER):
            settle_second(11, QUARTER * k + n, n)
        second_out(k).start()

    first_out.wait()
    for k in range(QUARTERS):
        second_out(k).wait()


def block_call(*operands):
    vmem = pl.BlockSpec(memory_space=pltpu.VMEM)
    smem = pl.BlockSpec(memory_space=pltpu.SMEM)
    hbm = pl.BlockSpec(memory_space=pl.ANY)
    m1 = 2 * I1 * SPAN + HALO_ROWS
    return pl.pallas_call(
        main_kernel,
        in_specs=[smem, vmem, vmem, vmem, vmem, hbm, hbm, hbm],
        out_specs=[hbm, hbm],
        out_shape=[
            jax.ShapeDtypeStruct((2, ROWS, COLS, C), BF),
            jax.ShapeDtypeStruct((SETS, K3, C), BF),
        ],
        scratch_shapes=[
            pltpu.VMEM((9, 38 * 16, CELLS), BF),
            pltpu.VMEM((6, R1, 4, SPAN, C), BF),
            pltpu.VMEM((6, 2, HALO_ROWS + 8, K3), F32),
            pltpu.VMEM((R2, 4, SPAN, C), BF),
            pltpu.VMEM((R2, 4, SPAN, C), BF),
            pltpu.VMEM((R2, 4, SPAN, C), BF),
            pltpu.VMEM((R2, 4, SPAN, C), BF),
            pltpu.VMEM((2, R1, COLS, C), BF),
            pltpu.VMEM((4, 4, I1 * SPAN, C), BF),
            pltpu.VMEM((4, 4, I1 * SPAN, C), BF),
            pltpu.VMEM((4, HALO_ROWS, K3), BF),
            pltpu.VMEM((4, HALO_ROWS, K3), BF),
            pltpu.VMEM((4, m1, C), F32),
            pltpu.VMEM((4, m1, C), F32),
            pltpu.VMEM((2, 2, m1, C), F32),
            pltpu.VMEM((2, 4, K3, C), BF),
            pltpu.VMEM((ENTRY_ROWS, USED, C), F32),
            pltpu.VMEM((2 * QUARTER, 3, COLS, 128), F32),
            pltpu.VMEM((2, HALO_ROWS, C), F32),
            pltpu.VMEM((USED, 128), F32),
            pltpu.VMEM((QUARTERS, 3, 3, PIECE, C), BF),
            pltpu.VMEM((QUARTERS, SETS, PIECE, C), BF),
            pltpu.VMEM((2, ROWS, COLS, C), BF),
            pltpu.SemaphoreType.DMA((2, 3)),
            pltpu.SemaphoreType.DMA((QUARTERS,)),
            pltpu.SemaphoreType.DMA((QUARTERS,)),
            pltpu.SemaphoreType.DMA((QUARTERS + 1,)),
        ],
        compiler_params=pltpu.CompilerParams(vmem_limit_bytes=62 * MIB),
        name="block",
    )(*operands)[0]


def body(latent, clip_lengths, entry_kernel, first_gain, first_kernel, second_gain, second_kernel):
    everything, u1 = gathered(latent.transpose(0, 1, 3, 2), first_kernel)
    return block_call(
        clip_lengths,
        everything,
        entry_kernel.reshape(27 * 16, C),
        first_gain,
        second_gain,
        first_kernel.reshape(3, 3, K3, C),
        second_kernel.reshape(3, 3, K3, C),
        u1.reshape(SETS, K3, C),
    )


def solution(mesh):
    return jax.shard_map(
        body,
        mesh=mesh,
        in_specs=(P("tm", "sy", "sx", None), P(), P(), P(), P(), P(), P()),
        out_specs=P("tm", "sy", "sx", None),
        check_vma=False,
    )
```

```python
import functools

import jax
import jax.numpy as jnp
from jax import lax
from jax.experimental import pallas as pl
from jax.experimental.pallas import tpu as pltpu
from jax.sharding import PartitionSpec as P

C = 384
K3 = 3 * C
MIB = 2**20
BF = jnp.bfloat16
F32 = jnp.float32


MESH = pl.DeviceIdType.MESH
ROWS = 32
COLS = 32
HALO = 3
BAND = 16 + 2 * HALO
SOURCES = 4
WEIGHT_STEPS = 9
LAST = WEIGHT_STEPS - 1
PARTNERS = [(k, d) for k in range(SOURCES) for d in (0, 1, -1) if (k, d) != (0, 0)]
SENT = {0: (0, 16), 1: (16 - HALO, HALO), -1: (0, HALO)}
LANDS = {0: HALO, 1: 0, -1: HALO + 16}
SETS = 14
ENTERED = 1
LANDED = 6


def mix_weights(w, put):
    edge = [w[0][y] + w[2][y] for y in range(3)]
    times = [
        w[0],
        [(edge[y] + w[1][y]) * 0.5 for y in range(3)],
        [(edge[y] - w[1][y]) * 0.5 for y in range(3)],
        w[2],
        w[1],
    ]
    for t, g in enumerate(times):
        outer = g[0] + g[2]
        put(2 * t, (outer + g[1]) * 0.5)
        put(2 * t + 1, (outer - g[1]) * 0.5)
    for n, t in enumerate((1, 2)):
        put(10 + 2 * n, times[t][0])
        put(11 + 2 * n, times[t][2])


def weight_block(w_ref, u_ref):
    step = 16

    @pl.loop(0, w_ref.shape[3] // step)
    def _(block):
        part = pl.ds(pl.multiple_of(block * step, step), step)
        for lane in range(3):
            lanes = slice(lane * 128, (lane + 1) * 128)
            w = [[w_ref[t, y, 0, part, lanes].astype(F32) for y in range(3)] for t in range(3)]

            def put(n, value, lanes=lanes):
                u_ref[n, 0, part, lanes] = value.astype(BF)

            mix_weights(w, put)


def gather_kernel(
    latent_ref, w1_ref, all_ref, u1_ref, own_ref, send_sem, recv_sem, local_sem, pair_sem
):
    step = pl.program_id(0)
    tm = lax.axis_index("tm")
    sy = lax.axis_index("sy")
    sx = lax.axis_index("sx")
    tms = lax.axis_size("tm")
    sys = lax.axis_size("sy")

    def place(k, d):
        return (lax.rem(tm + k + tms, tms), lax.rem(sy + d + sys, sys), sx)

    def copy(n):
        k, d = PARTNERS[n]
        first, count = SENT[d]
        return pltpu.make_async_remote_copy(
            src_ref=own_ref.at[pl.ds(first, count)],
            dst_ref=all_ref.at[SOURCES - 1 - k, sx, pl.ds(LANDS[d], count)],
            send_sem=send_sem.at[n],
            recv_sem=recv_sem.at[n],
            device_id=place(k, d),
            device_id_type=MESH,
        )

    def local():
        return pltpu.make_async_copy(
            own_ref, all_ref.at[SOURCES - 1, sx, pl.ds(HALO, 16)], local_sem
        )

    def across():
        return pltpu.make_async_remote_copy(
            src_ref=all_ref.at[:, sx],
            dst_ref=all_ref.at[:, sx],
            send_sem=pair_sem.at[0],
            recv_sem=pair_sem.at[1],
            device_id=(tm, sy, 1 - sx),
            device_id_type=MESH,
        )

    @pl.when(step == 0)
    def _():
        barrier = pltpu.get_barrier_semaphore()
        for k, d in PARTNERS:
            pl.semaphore_signal(barrier, inc=1, device_id=place(-k, -d), device_id_type=MESH)
        pl.semaphore_signal(barrier, inc=1, device_id=(tm, sy, 1 - sx), device_id_type=MESH)
        line = lax.broadcasted_iota(jnp.int32, (COLS, 128), 0)
        lane = lax.broadcasted_iota(jnp.int32, (COLS, 128), 1)
        packed = jnp.zeros((16 * 16, 128), F32)
        for half in range(2):
            for f in range(2):
                to = jnp.where(lane == line + (2 * half + f) * COLS, 1.0, 0.0).astype(BF)
                rows = latent_ref[f, half * 16 : (half + 1) * 16].reshape(16 * 16, COLS)
                packed = packed + jnp.dot(rows, to, preferred_element_type=F32)
        own_ref[...] = packed.astype(BF).reshape(16, 16, 128)
        local().start()

    @pl.when(step == ENTERED)
    def _():
        pl.semaphore_wait(pltpu.get_barrier_semaphore(), len(PARTNERS) + 1)
        for n in range(len(PARTNERS)):
            copy(n).start()

    weight_block(w1_ref, u1_ref)

    @pl.when(step == LANDED)
    def _():
        local().wait()
        for n in range(len(PARTNERS)):
            copy(n).wait()
        across().start()

    @pl.when(step == LAST)
    def _():
        across().wait()


def gathered(latent, first_kernel):
    chunk = C // 3
    hbm = pl.BlockSpec(memory_space=pl.ANY)
    copies = len(PARTNERS)
    return pl.pallas_call(
        gather_kernel,
        grid=(WEIGHT_STEPS,),
        in_specs=[
            pl.BlockSpec(memory_space=pltpu.VMEM),
            pl.BlockSpec((3, 3, 1, chunk, C), lambda step: (0, 0, step // 3, step % 3, 0)),
        ],
        out_specs=[
            hbm,
            pl.BlockSpec((SETS, 1, chunk, C), lambda step: (0, step // 3, step % 3, 0)),
        ],
        out_shape=[
            jax.ShapeDtypeStruct((SOURCES, 2, BAND, 16, 128), BF),
            jax.ShapeDtypeStruct((SETS, 3, C, C), BF),
        ],
        scratch_shapes=[
            pltpu.VMEM((16, 16, 128), BF),
            pltpu.SemaphoreType.DMA((copies,)),
            pltpu.SemaphoreType.DMA((copies,)),
            pltpu.SemaphoreType.DMA,
            pltpu.SemaphoreType.DMA((2,)),
        ],
        compiler_params=pltpu.CompilerParams(
            vmem_limit_bytes=62 * MIB, collective_id=0, has_side_effects=True
        ),
        cost_estimate=pl.CostEstimate(
            flops=60 * 9 * C * C, bytes_accessed=41 * 3 * C * C * 2, transcendentals=0
        ),
        name="gather",
    )(latent, first_kernel)


WIDE = 40
LEAD = 9
SPAN = 16
CELLS = 256
USED = 6 * 2 * SPAN + 24
INNER = 6 * 2 * SPAN
R1 = ROWS + 4
R2 = ROWS + 2
I1 = R2 // 2
I2 = ROWS // 2
HALO_ROWS = 32
ENTRY_ROWS = 12
QUARTER = 4
QUARTERS = 4
PIECE = 48
PIECES = K3 // PIECE
AHEAD = 3


def norm_act(values, gain, keep):
    mean = jnp.mean(values * values, axis=-1, keepdims=True)
    half = values * (lax.rsqrt(mean + 1e-6) * keep) * gain
    return half * jnp.tanh(half) + half


def norm_act_wide(values, gain, keep):
    squares = values * values
    folded = squares[:, :128] + squares[:, 128:256] + squares[:, 256:]
    ones = jnp.full((128, 128), 1.0, BF)
    mean = jnp.dot(folded.astype(BF), ones, preferred_element_type=F32) * (1.0 / C)
    scale = lax.rsqrt(mean + 1e-6) * keep
    half = values * jnp.concatenate([scale] * 3, axis=1) * gain
    return half * jnp.tanh(half) + half


def shifted(values, edge, ahead):
    line = lax.broadcasted_iota(jnp.int32, values.shape, 0)
    if ahead:
        return jnp.where(line == SPAN - 1, edge, pltpu.roll(values, SPAN - 1, axis=0))
    return jnp.where(line == 0, edge, pltpu.roll(values, 1, axis=0))


def clip_scalars(lengths, first, count):
    found = [jnp.int32(0)] * count
    start = jnp.int32(0)
    for k in range(lengths.shape[0]):
        for n in range(count):
            t = first + n
            found[n] = jnp.where(start <= t, t - start, found[n])
        start = start + lengths[k]
    return found


def spread_latents(all_ref, q_ref, distance, sx, top, bottom):
    depth = SOURCES * 2 * 128
    index = lax.broadcasted_iota(jnp.int32, (depth, 1), 0)
    source = index // 256
    side = (index // 128) % 2
    half = (index // 64) % 2
    frame = (index // 32) % 2
    x = index % 32
    column = jnp.where(side == sx, x, jnp.where(sx == 0, x + COLS, x - COLS))
    wanted = (column >= -HALO) & (column < COLS + HALO)
    target = (2 * source + frame) * WIDE + column + LEAD + 1
    lane = lax.broadcasted_iota(jnp.int32, (depth, 384), 1)
    spread = []
    for h in range(2):
        to = jnp.where(wanted & (half == h), target, -1)
        pick = jnp.where(lane == to, 1.0, 0.0).astype(BF)
        bands = (0, 16 + HALO) if h else (HALO, BAND)
        rows = (bands[1] - bands[0]) * 16
        lhs = jnp.concatenate(
            [
                all_ref[t, s, bands[0] : bands[1]].reshape(rows, 128)
                for t in range(SOURCES)
                for s in range(2)
            ],
            axis=1,
        )
        spread.append(jnp.dot(lhs, pick, preferred_element_type=F32))
    lower, upper = spread
    edge = HALO * 16
    pt = jnp.concatenate(
        [
            upper[:edge] * top.astype(F32),
            lower[: 16 * 16],
            upper[edge:],
            lower[16 * 16 :] * bottom.astype(F32),
        ],
        axis=0,
    )
    pt = pt.astype(BF)
    cell = lax.broadcasted_iota(jnp.int32, (1, CELLS), 1)
    beyond = cell - INNER
    halo = beyond // 6
    frame_of = jnp.where(cell < INNER, cell // 32, beyond - 6 * halo)
    column = jnp.where(
        cell < INNER,
        2 * (cell % SPAN) + (cell // SPAN) % 2,
        jnp.where(halo < 2, halo - 2, COLS + halo - 2),
    )
    base = frame_of * WIDE + column + LEAD
    line = lax.broadcasted_iota(jnp.int32, (384, CELLS), 0)
    for lag in range(3):
        keep = jnp.zeros((1, CELLS), jnp.int32)
        for f in range(6):
            keep = jnp.where(frame_of == f, (distance[f] >= lag).astype(jnp.int32), keep)
        keep = jnp.where(cell < USED, keep, 0)
        for dx in range(3):
            to = jnp.where(keep == 1, base + (2 - lag) * WIDE + dx, -1)
            pick = jnp.where(line == to, 1.0, 0.0).astype(BF)
            q_ref[3 * lag + dx] = jnp.dot(pt, pick, preferred_element_type=F32).astype(BF)


def main_kernel(
    lengths, all_ref, we_ref, g1_ref, g2_ref, w1_hbm, w2_hbm, u1_hbm,
    out_hbm, u2_hbm,
    q_ref, f_ref, h_ref, s0_ref, s1_ref, s2_ref, s3_ref, e_ref, xa_ref, xb_ref, hxa_ref, hxb_ref, ma_ref, mb_ref, acc_ref,
    w_ref, a_ref, b_ref, hn_ref, keep_ref, raw_ref, made_ref, out_ref, sem, raw_sem, made_sem,
    out_sem,
):
    tm = lax.axis_index("tm")
    sy = lax.axis_index("sy")
    sx = lax.axis_index("sx")
    top = (sy > 0).astype(jnp.int32)
    bottom = (sy < lax.axis_size("sy") - 1).astype(jnp.int32)
    left = sx == 0
    distance = clip_scalars(lengths, 2 * tm - 4, 6)
    s_refs = (s0_ref, s1_ref, s2_ref, s3_ref)
    x_refs, hx_refs, m_refs = (xa_ref, xb_ref), (hxa_ref, hxb_ref), (ma_ref, mb_ref)

    def pair_of(step):
        n = (0, 1, 1)[step // 4]
        whole = distance[3 + 2 * n] >= 1
        return (
            (distance[2 + 2 * n] >= 2).astype(F32),
            (distance[2 + 2 * n] >= 1).astype(F32),
            whole.astype(F32),
            whole,
        )

    def weight_copies(step):
        slot, tau = step % 2, step % 4
        w_hbm, u_hbm = (w1_hbm, u1_hbm) if step < 8 else (w2_hbm, u2_hbm)
        whole = pair_of(step)[3]
        which = (0, jnp.where(whole, 1, 4), jnp.where(whole, 2, 3), 3)[tau]
        mixed = pltpu.make_async_copy(
            u_hbm.at[pl.ds(2 * which, 2)], w_ref.at[slot, pl.ds(1, 2)], sem.at[slot, 0]
        )

        def outer(source, n):
            return pltpu.make_async_copy(source, w_ref.at[slot, 3 * n], sem.at[slot, 1 + n])

        tap = (0, 1, 2, 2)[tau]
        plain = [outer(w_hbm.at[tap, 2 * n], n) for n in range(2)]
        made = None
        if tau in (1, 2):
            made = [outer(u_hbm.at[8 + 2 * tau + n], n) for n in range(2)]
        return whole, mixed, plain, made

    def fetch(step):
        whole, mixed, plain, made = weight_copies(step)
        mixed.start()
        if made is None:
            for one in plain:
                one.start()
            return

        @pl.when(whole)
        def _():
            for one in made:
                one.start()

        @pl.when(jnp.logical_not(whole))
        def _():
            for one in plain:
                one.start()

    def arrive(step):
        _, mixed, plain, _ = weight_copies(step)
        mixed.wait()
        for one in plain:
            one.wait()

    def raw_copy(piece, slot):
        part = pl.ds(pl.multiple_of(piece * PIECE, PIECE), PIECE)
        return pltpu.make_async_copy(w2_hbm.at[:, :, part], raw_ref.at[slot], raw_sem.at[slot])

    def made_copy(piece, slot):
        part = pl.ds(pl.multiple_of(piece * PIECE, PIECE), PIECE)
        return pltpu.make_async_copy(made_ref.at[slot], u2_hbm.at[:, part], made_sem.at[slot])

    def piece_in(step, k):
        piece = QUARTERS * step + k
        raw_copy(piece, k).wait()
        if step > 0:
            made_copy(piece - QUARTERS, k).wait()
        if step < PIECES // QUARTERS - 1:
            raw_copy(piece + AHEAD, lax.rem(k + AHEAD, QUARTERS)).start()
        else:

            @pl.when(k + AHEAD < QUARTERS)
            def _():
                raw_copy(piece + AHEAD, lax.rem(k + AHEAD, QUARTERS)).start()

    def piece_made(step, k):
        slot = k
        for block in range(PIECE // 16):
            rows = slice(block * 16, (block + 1) * 16)
            for lane in range(3):
                lanes = slice(lane * 128, (lane + 1) * 128)
                w = [
                    [raw_ref[slot, t, y, rows, lanes] for y in range(3)]
                    for t in range(3)
                ]

                def put(n, value, rows=rows, lanes=lanes):
                    made_ref[slot, n, rows, lanes] = value

                mix_weights(w, put)

    def piece_out(step, k):
        made_copy(QUARTERS * step + k, k).start()

    fetch(0)
    for k in range(AHEAD):
        raw_copy(k, k).start()
    spread_latents(all_ref, q_ref, distance, sx, top, bottom)
    cell = lax.broadcasted_iota(jnp.int32, (USED, 128), 0)
    off_left = (cell >= INNER) & (cell < INNER + 12)
    off_right = cell >= INNER + 12
    keep_ref[...] = jnp.where((off_left & left) | (off_right & (sx == 1)), 0.0, 1.0)
    first_gain = g1_ref[...][None, :] * 0.5
    second_gain = g2_ref[...][None, :] * 0.5
    h_ref[...] = jnp.zeros_like(h_ref)

    @pl.loop(0, R1 // ENTRY_ROWS)
    def _(block):
        cols = []
        for n in range(ENTRY_ROWS):
            first = pl.multiple_of((block * ENTRY_ROWS + n) * 16, 16)
            cols.append(
                jnp.concatenate(
                    [
                        q_ref[3 * lag + dx, pl.ds(first + 16 * dy, 16), :]
                        for lag in (2, 1, 0)
                        for dy in range(3)
                        for dx in range(3)
                    ],
                    axis=0,
                )
            )
        patches = jnp.concatenate(cols, axis=1)
        entry = lax.dot_general(
            patches, we_ref[...], (((0,), (0,)), ((), ())), preferred_element_type=F32
        ).astype(BF)
        for n in range(ENTRY_ROWS):
            row = block * ENTRY_ROWS + n
            inside = jnp.where(row < 2, top, jnp.where(row >= R1 - 2, bottom, 1)).astype(F32)
            value = entry[n * CELLS : n * CELLS + USED].astype(F32)
            for f in range(2):
                e_ref[f, row] = entry[n * CELLS + (4 + f) * 32 : n * CELLS + (5 + f) * 32]
            a_ref[n] = norm_act_wide(value, first_gain, keep_ref[...] * inside)
        for n in range(ENTRY_ROWS):
            row = block * ENTRY_ROWS + n
            for f in range(6):
                even = a_ref[n, f * 32 : f * 32 + SPAN, :]
                odd = a_ref[n, f * 32 + SPAN : f * 32 + 2 * SPAN, :]
                before = a_ref[n, INNER + 6 + f : INNER + 7 + f, :]
                after = a_ref[n, INNER + 12 + f : INNER + 13 + f, :]
                f_ref[f, row, 0] = shifted(odd, before, False).astype(BF)
                f_ref[f, row, 1] = even.astype(BF)
                f_ref[f, row, 2] = odd.astype(BF)
                f_ref[f, row, 3] = shifted(even, after, True).astype(BF)
                places = (
                    jnp.where(left, f * 32 + 31, INNER + f),
                    jnp.where(left, INNER + 12 + f, INNER + 6 + f),
                    jnp.where(left, INNER + 18 + f, f * 32),
                )
                for dx, place in enumerate(places):
                    h_ref[f, n % 2, pl.ds(row // 2, 1), dx * C : (dx + 1) * C] = a_ref[
                        n, pl.ds(place, 1), :
                    ]

    def time_mix(step, one, dtype):
        tau = step % 4
        k0, k1, s, _ = pair_of(step)
        base = 2 if 4 <= step < 8 else 0

        def scaled(value, by):
            if dtype == F32:
                return value * by
            tile = jnp.full((16, 128), by, F32).astype(BF)
            return value * jnp.tile(tile, (1, value.shape[1] // 128))

        if tau == 0:
            return scaled(one(base), k0) - scaled(one(base + 2), s)
        if tau == 1:
            return scaled(one(base + 1), k1) + scaled(one(base + 2), s)
        if tau == 2:
            return one(base + 2) - scaled(one(base + 1), s * k1)
        return scaled(one(base + 1), s * k1) - one(base + 3)

    def row_transform(d):
        return d[0] - d[2], d[1] + d[2], d[2] - d[1], d[1] - d[3]

    def build(step, i, count=1):
        def read(frame, row, j):
            return f_ref[frame, row, j] if step < 8 else s_refs[frame][row, j]

        x_ref = x_refs[step % 2]
        for j in range(4):
            d = [
                time_mix(step, lambda frame, k=k: read(frame, 2 * i + k, j), BF)
                for k in range(2 * count + 2)
            ]
            for n in range(count):
                part = pl.ds(pl.multiple_of((i + n) * SPAN, SPAN), SPAN)
                for k, value in enumerate(row_transform(d[2 * n : 2 * n + 4])):
                    x_ref[k, j, part, :] = value

    def build_halo(step):
        hx_ref = hx_refs[step % 2]
        for dx in range(3):
            lanes = slice(dx * C, (dx + 1) * C)
            d = [
                time_mix(
                    step,
                    lambda frame, k=k: h_ref[frame, k % 2, pl.ds(k // 2, HALO_ROWS), lanes],
                    F32,
                )
                for k in range(4)
            ]
            for k, value in enumerate(row_transform(d)):
                hx_ref[k, :, lanes] = value.astype(BF)

    def settle(step, part):
        tau = step % 4
        m_ref = m_refs[step % 2]
        s = pair_of(step)[2]
        t = [m_ref[k, part, :] for k in range(4)]
        middle = t[1] - t[2]
        both = (t[0] + t[1] + t[2], middle - t[3])
        if tau == 3:
            return 1, [acc_ref[1, p, part, :] - both[p] for p in range(2)]
        if tau == 2:
            for p in range(2):
                acc_ref[1, p, part, :] = acc_ref[1, p, part, :] - s * both[p]
            return 0, [acc_ref[0, p, part, :] + both[p] for p in range(2)]
        for p in range(2):
            if tau == 0:
                acc_ref[0, p, part, :] = both[p]
            else:
                acc_ref[0, p, part, :] = acc_ref[0, p, part, :] + both[p]
                acc_ref[1, p, part, :] = s * both[p]
        return None

    def settle_halo(step):
        done = settle(step, pl.ds(2 * I1 * SPAN, HALO_ROWS))
        if done is not None:
            for p, value in enumerate(done[1]):
                hn_ref[p] = norm_act(value, second_gain, 1.0)

    def settle_first(step, i):
        for side in range(2):
            first = pl.multiple_of(side * I1 * SPAN + i * SPAN, SPAN)
            done = settle(step, pl.ds(first, SPAN))
            if done is None:
                continue
            frame = 2 * (step // 4) + done[0]
            for p, value in enumerate(done[1]):
                row = 2 * i + p
                inside = jnp.where(row == 0, top, jnp.where(row == R2 - 1, bottom, 1)).astype(F32)
                value = norm_act(value, second_gain, inside)
                here = inside * jnp.where(sx == side, 1.0, 0.0)
                edge = hn_ref[p, pl.ds(i, 1), :] * here
                if side == 0:
                    s_refs[frame][row, 1] = value.astype(BF)
                    s_refs[frame][row, 3] = shifted(value, edge, True).astype(BF)
                else:
                    s_refs[frame][row, 2] = value.astype(BF)
                    s_refs[frame][row, 0] = shifted(value, edge, False).astype(BF)

    def settle_second(step, i, n):
        done = [
            settle(step, pl.ds(pl.multiple_of(side * I2 * SPAN + i * SPAN, SPAN), SPAN))
            for side in range(2)
        ]
        if done[0] is None:
            return
        member = done[0][0]
        for p in range(2):
            row = 2 * i + p
            for side in range(2):
                part = slice(side * SPAN, (side + 1) * SPAN)
                value = done[side][1][p] + e_ref[member, row + 2, part, :].astype(F32)
                for lane in range(3):
                    b_ref[2 * n + p, lane, pl.ds(side, SPAN, stride=2), :] = value[
                        :, lane * 128 : (lane + 1) * 128
                    ]
            for lane in range(3):
                out_ref[member, row, :, lane * 128 : (lane + 1) * 128] = b_ref[
                    2 * n + p, lane
                ].astype(BF)

    def products(step, k):
        x_ref, m_ref = x_refs[step % 2], m_refs[step % 2]
        count = (I1 if step < 8 else I2) * SPAN
        x = [x_ref[k, j, :count, :] for j in range(4)]
        even, odd, both = [jnp.concatenate(part, axis=1) for part in (x[:3], x[1:], x)]
        if step < 8:
            halo = hx_refs[step % 2][k]
            even = jnp.concatenate([even, halo], axis=0)
            none = jnp.zeros((HALO_ROWS, C), BF)
            both = jnp.concatenate([both, jnp.concatenate([halo, none], axis=1)], axis=0)
        slot = step % 2
        none = jnp.zeros((C, 128), BF)
        shared = jnp.concatenate(
            [
                jnp.concatenate([w_ref[slot, k, :, 256:], none], axis=0),
                jnp.concatenate([none, w_ref[slot, k, :, :128]], axis=0),
            ],
            axis=1,
        )
        low = jnp.dot(even, w_ref[slot, k, :, :256], preferred_element_type=F32)
        middle = jnp.dot(both, shared, preferred_element_type=F32)
        high = jnp.dot(odd, w_ref[slot, k, :, 128:], preferred_element_type=F32)
        m_ref[k, :count, :256] = low[:count]
        m_ref[k, :count, 256:] = middle[:count, :128]
        m_ref[k, count : 2 * count, :128] = middle[:count, 128:]
        m_ref[k, count : 2 * count, 128:] = high
        if step < 8:
            m_ref[k, 2 * count : 2 * count + HALO_ROWS, :256] = low[count:]
            m_ref[k, 2 * count : 2 * count + HALO_ROWS, 256:] = middle[count:, :128]

    def run(step):
        arrive(step)
        if step < 11:
            fetch(step + 1)
        builds = step < 11
        settles = step > 0
        pieces = step < PIECES // QUARTERS
        if builds and step < 7:
            build(step + 1, I1 - 1)
            build_halo(step + 1)
        if settles and step < 9:
            settle_halo(step - 1)
            settle_first(step - 1, I1 - 1)

        @pl.loop(0, QUARTERS)
        def _(k):
            if pieces:
                piece_in(step, k)
            products(step, k)
            for n in range(QUARTER if settles else 0):
                if step < 9:
                    settle_first(step - 1, QUARTER * k + n)
                else:
                    settle_second(step - 1, QUARTER * k + n, n)
            if step == 7:
                for n in range(QUARTER):
                    build(8, jnp.maximum(QUARTER * k + n - 1, 0))
            elif builds:
                build(step + 1, QUARTER * k, QUARTER)
            if pieces:
                piece_made(step, k)
                piece_out(step, k)

        if step == PIECES // QUARTERS - 1:
            for k in range(QUARTERS):
                made_copy(QUARTERS * step + k, k).wait()
        if step == 7:
            build(8, I2 - 1)

    @pl.loop(0, I1)
    def _(i):
        build(0, i)

    build_halo(0)
    for step in range(12):
        run(step)

    first_out = pltpu.make_async_copy(out_ref.at[0], out_hbm.at[0], out_sem.at[QUARTERS])
    first_out.start()

    def second_out(k):
        rows = pl.ds(2 * QUARTER * k, 2 * QUARTER)
        return pltpu.make_async_copy(out_ref.at[1, rows], out_hbm.at[1, rows], out_sem.at[k])

    @pl.loop(0, QUARTERS)
    def _(k):
        for n in range(QUARTER):
            settle_second(11, QUARTER * k + n, n)
        second_out(k).start()

    first_out.wait()
    for k in range(QUARTERS):
        second_out(k).wait()


def block_call(*operands):
    vmem = pl.BlockSpec(memory_space=pltpu.VMEM)
    smem = pl.BlockSpec(memory_space=pltpu.SMEM)
    hbm = pl.BlockSpec(memory_space=pl.ANY)
    m1 = 2 * I1 * SPAN + HALO_ROWS
    return pl.pallas_call(
        main_kernel,
        in_specs=[smem, vmem, vmem, vmem, vmem, hbm, hbm, hbm],
        out_specs=[hbm, hbm],
        out_shape=[
            jax.ShapeDtypeStruct((2, ROWS, COLS, C), BF),
            jax.ShapeDtypeStruct((SETS, K3, C), BF),
        ],
        scratch_shapes=[
            pltpu.VMEM((9, 38 * 16, CELLS), BF),
            pltpu.VMEM((6, R1, 4, SPAN, C), BF),
            pltpu.VMEM((6, 2, HALO_ROWS + 8, K3), F32),
            pltpu.VMEM((R2, 4, SPAN, C), BF),
            pltpu.VMEM((R2, 4, SPAN, C), BF),
            pltpu.VMEM((R2, 4, SPAN, C), BF),
            pltpu.VMEM((R2, 4, SPAN, C), BF),
            pltpu.VMEM((2, R1, COLS, C), BF),
            pltpu.VMEM((4, 4, I1 * SPAN, C), BF),
            pltpu.VMEM((4, 4, I1 * SPAN, C), BF),
            pltpu.VMEM((4, HALO_ROWS, K3), BF),
            pltpu.VMEM((4, HALO_ROWS, K3), BF),
            pltpu.VMEM((4, m1, C), F32),
            pltpu.VMEM((4, m1, C), F32),
            pltpu.VMEM((2, 2, m1, C), F32),
            pltpu.VMEM((2, 4, K3, C), BF),
            pltpu.VMEM((ENTRY_ROWS, USED, C), F32),
            pltpu.VMEM((2 * QUARTER, 3, COLS, 128), F32),
            pltpu.VMEM((2, HALO_ROWS, C), F32),
            pltpu.VMEM((USED, 128), F32),
            pltpu.VMEM((QUARTERS, 3, 3, PIECE, C), BF),
            pltpu.VMEM((QUARTERS, SETS, PIECE, C), BF),
            pltpu.VMEM((2, ROWS, COLS, C), BF),
            pltpu.SemaphoreType.DMA((2, 3)),
            pltpu.SemaphoreType.DMA((QUARTERS,)),
            pltpu.SemaphoreType.DMA((QUARTERS,)),
            pltpu.SemaphoreType.DMA((QUARTERS + 1,)),
        ],
        compiler_params=pltpu.CompilerParams(vmem_limit_bytes=62 * MIB),
        name="block",
    )(*operands)[0]


def body(latent, clip_lengths, entry_kernel, first_gain, first_kernel, second_gain, second_kernel):
    everything, u1 = gathered(latent.transpose(0, 1, 3, 2), first_kernel)
    return block_call(
        clip_lengths,
        everything,
        entry_kernel.reshape(27 * 16, C),
        first_gain,
        second_gain,
        first_kernel.reshape(3, 3, K3, C),
        second_kernel.reshape(3, 3, K3, C),
        u1.reshape(SETS, K3, C),
    )


def solution(mesh):
    return jax.shard_map(
        body,
        mesh=mesh,
        in_specs=(P("tm", "sy", "sx", None), P(), P(), P(), P(), P(), P()),
        out_specs=P("tm", "sy", "sx", None),
        check_vma=False,
    )
```

```python
import functools

import jax
import jax.numpy as jnp
from jax import lax
from jax.experimental import pallas as pl
from jax.experimental.pallas import tpu as pltpu
from jax.sharding import PartitionSpec as P

C = 384
K3 = 3 * C
MIB = 2**20
BF = jnp.bfloat16
F32 = jnp.float32


MESH = pl.DeviceIdType.MESH
ROWS = 32
COLS = 32
HALO = 3
BAND = 16 + 2 * HALO
SOURCES = 4
WEIGHT_STEPS = 9
LAST = WEIGHT_STEPS - 1
PARTNERS = [(2, 0), (3, 0), (1, 0)] + [(k, d) for k in (2, 3, 1, 0) for d in (1, -1)]
SENT = {0: (0, 16), 1: (16 - HALO, HALO), -1: (0, HALO)}
LANDS = {0: HALO, 1: 0, -1: HALO + 16}
SETS = 14
ENTERED = 1
LANDED = 6


def mix_weights(w, put):
    edge = [w[0][y] + w[2][y] for y in range(3)]
    times = [
        w[0],
        [(edge[y] + w[1][y]) * 0.5 for y in range(3)],
        [(edge[y] - w[1][y]) * 0.5 for y in range(3)],
        w[2],
        w[1],
    ]
    for t, g in enumerate(times):
        outer = g[0] + g[2]
        put(2 * t, (outer + g[1]) * 0.5)
        put(2 * t + 1, (outer - g[1]) * 0.5)
    for n, t in enumerate((1, 2)):
        put(10 + 2 * n, times[t][0])
        put(11 + 2 * n, times[t][2])


def weight_block(w_ref, u_ref):
    step = 16

    @pl.loop(0, w_ref.shape[3] // step)
    def _(block):
        part = pl.ds(pl.multiple_of(block * step, step), step)
        for lane in range(3):
            lanes = slice(lane * 128, (lane + 1) * 128)
            w = [[w_ref[t, y, 0, part, lanes].astype(F32) for y in range(3)] for t in range(3)]

            def put(n, value, lanes=lanes):
                u_ref[n, 0, part, lanes] = value.astype(BF)

            mix_weights(w, put)


def gather_kernel(
    latent_ref, w1_ref, all_ref, u1_ref, own_ref, send_sem, recv_sem, local_sem, pair_sem
):
    step = pl.program_id(0)
    tm = lax.axis_index("tm")
    sy = lax.axis_index("sy")
    sx = lax.axis_index("sx")
    tms = lax.axis_size("tm")
    sys = lax.axis_size("sy")

    def place(k, d):
        return (lax.rem(tm + k + tms, tms), lax.rem(sy + d + sys, sys), sx)

    def copy(n):
        k, d = PARTNERS[n]
        first, count = SENT[d]
        return pltpu.make_async_remote_copy(
            src_ref=own_ref.at[pl.ds(first, count)],
            dst_ref=all_ref.at[SOURCES - 1 - k, sx, pl.ds(LANDS[d], count)],
            send_sem=send_sem.at[n],
            recv_sem=recv_sem.at[n],
            device_id=place(k, d),
            device_id_type=MESH,
        )

    def local():
        return pltpu.make_async_copy(
            own_ref, all_ref.at[SOURCES - 1, sx, pl.ds(HALO, 16)], local_sem
        )

    def across():
        return pltpu.make_async_remote_copy(
            src_ref=all_ref.at[:, sx],
            dst_ref=all_ref.at[:, sx],
            send_sem=pair_sem.at[0],
            recv_sem=pair_sem.at[1],
            device_id=(tm, sy, 1 - sx),
            device_id_type=MESH,
        )

    @pl.when(step == 0)
    def _():
        barrier = pltpu.get_barrier_semaphore()
        for k, d in PARTNERS:
            pl.semaphore_signal(barrier, inc=1, device_id=place(-k, -d), device_id_type=MESH)
        pl.semaphore_signal(barrier, inc=1, device_id=(tm, sy, 1 - sx), device_id_type=MESH)
        line = lax.broadcasted_iota(jnp.int32, (COLS, 128), 0)
        lane = lax.broadcasted_iota(jnp.int32, (COLS, 128), 1)
        packed = jnp.zeros((16 * 16, 128), F32)
        for half in range(2):
            for f in range(2):
                to = jnp.where(lane == line + (2 * half + f) * COLS, 1.0, 0.0).astype(BF)
                rows = latent_ref[f, half * 16 : (half + 1) * 16].reshape(16 * 16, COLS)
                packed = packed + jnp.dot(rows, to, preferred_element_type=F32)
        own_ref[...] = packed.astype(BF).reshape(16, 16, 128)
        local().start()

    @pl.when(step == ENTERED)
    def _():
        pl.semaphore_wait(pltpu.get_barrier_semaphore(), len(PARTNERS) + 1)
        for n in range(len(PARTNERS)):
            copy(n).start()

    weight_block(w1_ref, u1_ref)

    @pl.when(step == LANDED)
    def _():
        local().wait()
        for n in range(len(PARTNERS)):
            copy(n).wait()
        across().start()

    @pl.when(step == LAST)
    def _():
        across().wait()


def gathered(latent, first_kernel):
    chunk = C // 3
    hbm = pl.BlockSpec(memory_space=pl.ANY)
    copies = len(PARTNERS)
    return pl.pallas_call(
        gather_kernel,
        grid=(WEIGHT_STEPS,),
        in_specs=[
            pl.BlockSpec(memory_space=pltpu.VMEM),
            pl.BlockSpec((3, 3, 1, chunk, C), lambda step: (0, 0, step // 3, step % 3, 0)),
        ],
        out_specs=[
            hbm,
            pl.BlockSpec((SETS, 1, chunk, C), lambda step: (0, step // 3, step % 3, 0)),
        ],
        out_shape=[
            jax.ShapeDtypeStruct((SOURCES, 2, BAND, 16, 128), BF),
            jax.ShapeDtypeStruct((SETS, 3, C, C), BF),
        ],
        scratch_shapes=[
            pltpu.VMEM((16, 16, 128), BF),
            pltpu.SemaphoreType.DMA((copies,)),
            pltpu.SemaphoreType.DMA((copies,)),
            pltpu.SemaphoreType.DMA,
            pltpu.SemaphoreType.DMA((2,)),
        ],
        compiler_params=pltpu.CompilerParams(
            vmem_limit_bytes=62 * MIB, collective_id=0, has_side_effects=True
        ),
        cost_estimate=pl.CostEstimate(
            flops=60 * 9 * C * C, bytes_accessed=41 * 3 * C * C * 2, transcendentals=0
        ),
        name="gather",
    )(latent, first_kernel)


WIDE = 40
LEAD = 9
SPAN = 16
CELLS = 256
USED = 6 * 2 * SPAN + 24
INNER = 6 * 2 * SPAN
R1 = ROWS + 4
R2 = ROWS + 2
I1 = R2 // 2
I2 = ROWS // 2
HALO_ROWS = 32
ENTRY_ROWS = 12
QUARTER = 4
QUARTERS = 4
PIECE = 48
PIECES = K3 // PIECE
AHEAD = 3


def norm_act(values, gain, keep):
    mean = jnp.mean(values * values, axis=-1, keepdims=True)
    half = values * (lax.rsqrt(mean + 1e-6) * keep) * gain
    return half * jnp.tanh(half) + half


def norm_act_wide(values, gain, keep):
    squares = values * values
    folded = squares[:, :128] + squares[:, 128:256] + squares[:, 256:]
    ones = jnp.full((128, 128), 1.0, BF)
    mean = jnp.dot(folded.astype(BF), ones, preferred_element_type=F32) * (1.0 / C)
    scale = lax.rsqrt(mean + 1e-6) * keep
    half = values * jnp.concatenate([scale] * 3, axis=1) * gain
    return half * jnp.tanh(half) + half


def shifted(values, edge, ahead):
    line = lax.broadcasted_iota(jnp.int32, values.shape, 0)
    if ahead:
        return jnp.where(line == SPAN - 1, edge, pltpu.roll(values, SPAN - 1, axis=0))
    return jnp.where(line == 0, edge, pltpu.roll(values, 1, axis=0))


def clip_scalars(lengths, first, count):
    found = [jnp.int32(0)] * count
    start = jnp.int32(0)
    for k in range(lengths.shape[0]):
        for n in range(count):
            t = first + n
            found[n] = jnp.where(start <= t, t - start, found[n])
        start = start + lengths[k]
    return found


def spread_latents(all_ref, q_ref, distance, sx, top, bottom):
    depth = SOURCES * 2 * 128
    index = lax.broadcasted_iota(jnp.int32, (depth, 1), 0)
    source = index // 256
    side = (index // 128) % 2
    half = (index // 64) % 2
    frame = (index // 32) % 2
    x = index % 32
    column = jnp.where(side == sx, x, jnp.where(sx == 0, x + COLS, x - COLS))
    wanted = (column >= -HALO) & (column < COLS + HALO)
    target = (2 * source + frame) * WIDE + column + LEAD + 1
    lane = lax.broadcasted_iota(jnp.int32, (depth, 384), 1)
    spread = []
    for h in range(2):
        to = jnp.where(wanted & (half == h), target, -1)
        pick = jnp.where(lane == to, 1.0, 0.0).astype(BF)
        bands = (0, 16 + HALO) if h else (HALO, BAND)
        rows = (bands[1] - bands[0]) * 16
        lhs = jnp.concatenate(
            [
                all_ref[t, s, bands[0] : bands[1]].reshape(rows, 128)
                for t in range(SOURCES)
                for s in range(2)
            ],
            axis=1,
        )
        spread.append(jnp.dot(lhs, pick, preferred_element_type=F32))
    lower, upper = spread
    edge = HALO * 16
    pt = jnp.concatenate(
        [
            upper[:edge] * top.astype(F32),
            lower[: 16 * 16],
            upper[edge:],
            lower[16 * 16 :] * bottom.astype(F32),
        ],
        axis=0,
    )
    pt = pt.astype(BF)
    cell = lax.broadcasted_iota(jnp.int32, (1, CELLS), 1)
    beyond = cell - INNER
    halo = beyond // 6
    frame_of = jnp.where(cell < INNER, cell // 32, beyond - 6 * halo)
    column = jnp.where(
        cell < INNER,
        2 * (cell % SPAN) + (cell // SPAN) % 2,
        jnp.where(halo < 2, halo - 2, COLS + halo - 2),
    )
    base = frame_of * WIDE + column + LEAD
    line = lax.broadcasted_iota(jnp.int32, (384, CELLS), 0)
    for lag in range(3):
        keep = jnp.zeros((1, CELLS), jnp.int32)
        for f in range(6):
            keep = jnp.where(frame_of == f, (distance[f] >= lag).astype(jnp.int32), keep)
        keep = jnp.where(cell < USED, keep, 0)
        for dx in range(3):
            to = jnp.where(keep == 1, base + (2 - lag) * WIDE + dx, -1)
            pick = jnp.where(line == to, 1.0, 0.0).astype(BF)
            q_ref[3 * lag + dx] = jnp.dot(pt, pick, preferred_element_type=F32).astype(BF)


def main_kernel(
    lengths, all_ref, we_ref, g1_ref, g2_ref, w1_hbm, w2_hbm, u1_hbm,
    out_hbm, u2_hbm,
    q_ref, f_ref, h_ref, s0_ref, s1_ref, s2_ref, s3_ref, e_ref, xa_ref, xb_ref, hxa_ref, hxb_ref, ma_ref, mb_ref, acc_ref,
    w_ref, a_ref, b_ref, hn_ref, keep_ref, raw_ref, made_ref, out_ref, sem, raw_sem, made_sem,
    out_sem,
):
    tm = lax.axis_index("tm")
    sy = lax.axis_index("sy")
    sx = lax.axis_index("sx")
    top = (sy > 0).astype(jnp.int32)
    bottom = (sy < lax.axis_size("sy") - 1).astype(jnp.int32)
    left = sx == 0
    distance = clip_scalars(lengths, 2 * tm - 4, 6)
    s_refs = (s0_ref, s1_ref, s2_ref, s3_ref)
    x_refs, hx_refs, m_refs = (xa_ref, xb_ref), (hxa_ref, hxb_ref), (ma_ref, mb_ref)

    def pair_of(step):
        n = (0, 1, 1)[step // 4]
        whole = distance[3 + 2 * n] >= 1
        return (
            (distance[2 + 2 * n] >= 2).astype(F32),
            (distance[2 + 2 * n] >= 1).astype(F32),
            whole.astype(F32),
            whole,
        )

    def weight_copies(step):
        slot, tau = step % 2, step % 4
        w_hbm, u_hbm = (w1_hbm, u1_hbm) if step < 8 else (w2_hbm, u2_hbm)
        whole = pair_of(step)[3]
        which = (0, jnp.where(whole, 1, 4), jnp.where(whole, 2, 3), 3)[tau]
        mixed = pltpu.make_async_copy(
            u_hbm.at[pl.ds(2 * which, 2)], w_ref.at[slot, pl.ds(1, 2)], sem.at[slot, 0]
        )

        def outer(source, n):
            return pltpu.make_async_copy(source, w_ref.at[slot, 3 * n], sem.at[slot, 1 + n])

        tap = (0, 1, 2, 2)[tau]
        plain = [outer(w_hbm.at[tap, 2 * n], n) for n in range(2)]
        made = None
        if tau in (1, 2):
            made = [outer(u_hbm.at[8 + 2 * tau + n], n) for n in range(2)]
        return whole, mixed, plain, made

    def fetch(step):
        whole, mixed, plain, made = weight_copies(step)
        mixed.start()
        if made is None:
            for one in plain:
                one.start()
            return

        @pl.when(whole)
        def _():
            for one in made:
                one.start()

        @pl.when(jnp.logical_not(whole))
        def _():
            for one in plain:
                one.start()

    def arrive(step):
        _, mixed, plain, _ = weight_copies(step)
        mixed.wait()
        for one in plain:
            one.wait()

    def raw_copy(piece, slot):
        part = pl.ds(pl.multiple_of(piece * PIECE, PIECE), PIECE)
        return pltpu.make_async_copy(w2_hbm.at[:, :, part], raw_ref.at[slot], raw_sem.at[slot])

    def made_copy(piece, slot):
        part = pl.ds(pl.multiple_of(piece * PIECE, PIECE), PIECE)
        return pltpu.make_async_copy(made_ref.at[slot], u2_hbm.at[:, part], made_sem.at[slot])

    def piece_in(step, k):
        piece = QUARTERS * step + k
        raw_copy(piece, k).wait()
        if step > 0:
            made_copy(piece - QUARTERS, k).wait()
        if step < PIECES // QUARTERS - 1:
            raw_copy(piece + AHEAD, lax.rem(k + AHEAD, QUARTERS)).start()
        else:

            @pl.when(k + AHEAD < QUARTERS)
            def _():
                raw_copy(piece + AHEAD, lax.rem(k + AHEAD, QUARTERS)).start()

    def piece_made(step, k):
        slot = k
        for block in range(PIECE // 16):
            rows = slice(block * 16, (block + 1) * 16)
            for lane in range(3):
                lanes = slice(lane * 128, (lane + 1) * 128)
                w = [
                    [raw_ref[slot, t, y, rows, lanes] for y in range(3)]
                    for t in range(3)
                ]

                def put(n, value, rows=rows, lanes=lanes):
                    made_ref[slot, n, rows, lanes] = value

                mix_weights(w, put)

    def piece_out(step, k):
        made_copy(QUARTERS * step + k, k).start()

    fetch(0)
    for k in range(AHEAD):
        raw_copy(k, k).start()
    spread_latents(all_ref, q_ref, distance, sx, top, bottom)
    cell = lax.broadcasted_iota(jnp.int32, (USED, 128), 0)
    off_left = (cell >= INNER) & (cell < INNER + 12)
    off_right = cell >= INNER + 12
    keep_ref[...] = jnp.where((off_left & left) | (off_right & (sx == 1)), 0.0, 1.0)
    first_gain = g1_ref[...][None, :] * 0.5
    second_gain = g2_ref[...][None, :] * 0.5
    h_ref[...] = jnp.zeros_like(h_ref)

    @pl.loop(0, R1 // ENTRY_ROWS)
    def _(block):
        cols = []
        for n in range(ENTRY_ROWS):
            first = pl.multiple_of((block * ENTRY_ROWS + n) * 16, 16)
            cols.append(
                jnp.concatenate(
                    [
                        q_ref[3 * lag + dx, pl.ds(first + 16 * dy, 16), :]
                        for lag in (2, 1, 0)
                        for dy in range(3)
                        for dx in range(3)
                    ],
                    axis=0,
                )
            )
        patches = jnp.concatenate(cols, axis=1)
        entry = lax.dot_general(
            patches, we_ref[...], (((0,), (0,)), ((), ())), preferred_element_type=F32
        ).astype(BF)
        for n in range(ENTRY_ROWS):
            row = block * ENTRY_ROWS + n
            inside = jnp.where(row < 2, top, jnp.where(row >= R1 - 2, bottom, 1)).astype(F32)
            value = entry[n * CELLS : n * CELLS + USED].astype(F32)
            for f in range(2):
                e_ref[f, row] = entry[n * CELLS + (4 + f) * 32 : n * CELLS + (5 + f) * 32]
            a_ref[n] = norm_act_wide(value, first_gain, keep_ref[...] * inside)
        for n in range(ENTRY_ROWS):
            row = block * ENTRY_ROWS + n
            for f in range(6):
                even = a_ref[n, f * 32 : f * 32 + SPAN, :]
                odd = a_ref[n, f * 32 + SPAN : f * 32 + 2 * SPAN, :]
                before = a_ref[n, INNER + 6 + f : INNER + 7 + f, :]
                after = a_ref[n, INNER + 12 + f : INNER + 13 + f, :]
                f_ref[f, row, 0] = shifted(odd, before, False).astype(BF)
                f_ref[f, row, 1] = even.astype(BF)
                f_ref[f, row, 2] = odd.astype(BF)
                f_ref[f, row, 3] = shifted(even, after, True).astype(BF)
                places = (
                    jnp.where(left, f * 32 + 31, INNER + f),
                    jnp.where(left, INNER + 12 + f, INNER + 6 + f),
                    jnp.where(left, INNER + 18 + f, f * 32),
                )
                for dx, place in enumerate(places):
                    h_ref[f, n % 2, pl.ds(row // 2, 1), dx * C : (dx + 1) * C] = a_ref[
                        n, pl.ds(place, 1), :
                    ]

    def time_mix(step, one, dtype):
        tau = step % 4
        k0, k1, s, _ = pair_of(step)
        base = 2 if 4 <= step < 8 else 0

        def scaled(value, by):
            if dtype == F32:
                return value * by
            tile = jnp.full((16, 128), by, F32).astype(BF)
            return value * jnp.tile(tile, (1, value.shape[1] // 128))

        if tau == 0:
            return scaled(one(base), k0) - scaled(one(base + 2), s)
        if tau == 1:
            return scaled(one(base + 1), k1) + scaled(one(base + 2), s)
        if tau == 2:
            return one(base + 2) - scaled(one(base + 1), s * k1)
        return scaled(one(base + 1), s * k1) - one(base + 3)

    def row_transform(d):
        return d[0] - d[2], d[1] + d[2], d[2] - d[1], d[1] - d[3]

    def build(step, i, count=1):
        def read(frame, row, j):
            return f_ref[frame, row, j] if step < 8 else s_refs[frame][row, j]

        x_ref = x_refs[step % 2]
        for j in range(4):
            d = [
                time_mix(step, lambda frame, k=k: read(frame, 2 * i + k, j), BF)
                for k in range(2 * count + 2)
            ]
            for n in range(count):
                part = pl.ds(pl.multiple_of((i + n) * SPAN, SPAN), SPAN)
                for k, value in enumerate(row_transform(d[2 * n : 2 * n + 4])):
                    x_ref[k, j, part, :] = value

    def build_halo(step, quarter):
        hx_ref = hx_refs[step % 2]
        first = pl.multiple_of(8 * quarter, 8)
        read = pl.multiple_of(jnp.minimum(8 * quarter, 16), 8)
        for dx in range(3):
            lanes = slice(dx * C, (dx + 1) * C)
            both = [
                time_mix(
                    step, lambda frame, p=p: h_ref[frame, p, pl.ds(read, 16), lanes], F32
                )
                for p in range(2)
            ]
            d = [both[0][:8], both[1][:8], both[0][1:9], both[1][1:9]]
            for k, value in enumerate(row_transform(d)):
                hx_ref[k, pl.ds(first, 8), lanes] = value

    def settle(step, part):
        tau = step % 4
        m_ref = m_refs[step % 2]
        s = pair_of(step)[2]
        t = [m_ref[k, part, :] for k in range(4)]
        middle = t[1] - t[2]
        both = (t[0] + t[1] + t[2], middle - t[3])
        if tau == 3:
            return 1, [acc_ref[1, p, part, :] - both[p] for p in range(2)]
        if tau == 2:
            for p in range(2):
                acc_ref[1, p, part, :] = acc_ref[1, p, part, :] - s * both[p]
            return 0, [acc_ref[0, p, part, :] + both[p] for p in range(2)]
        for p in range(2):
            if tau == 0:
                acc_ref[0, p, part, :] = both[p]
            else:
                acc_ref[0, p, part, :] = acc_ref[0, p, part, :] + both[p]
                acc_ref[1, p, part, :] = s * both[p]
        return None

    def settle_halo(step):
        done = settle(step, pl.ds(2 * I1 * SPAN, HALO_ROWS))
        if done is not None:
            for p, value in enumerate(done[1]):
                hn_ref[p] = norm_act(value, second_gain, 1.0)

    def settle_first(step, i):
        for side in range(2):
            first = pl.multiple_of(side * I1 * SPAN + i * SPAN, SPAN)
            done = settle(step, pl.ds(first, SPAN))
            if done is None:
                continue
            frame = 2 * (step // 4) + done[0]
            for p, value in enumerate(done[1]):
                row = 2 * i + p
                inside = jnp.where(row == 0, top, jnp.where(row == R2 - 1, bottom, 1)).astype(F32)
                value = norm_act(value, second_gain, inside)
                here = inside * jnp.where(sx == side, 1.0, 0.0)
                edge = hn_ref[p, pl.ds(i, 1), :] * here
                if side == 0:
                    s_refs[frame][row, 1] = value.astype(BF)
                    s_refs[frame][row, 3] = shifted(value, edge, True).astype(BF)
                else:
                    s_refs[frame][row, 2] = value.astype(BF)
                    s_refs[frame][row, 0] = shifted(value, edge, False).astype(BF)

    def settle_second(step, i, n):
        done = [
            settle(step, pl.ds(pl.multiple_of(side * I2 * SPAN + i * SPAN, SPAN), SPAN))
            for side in range(2)
        ]
        if done[0] is None:
            return
        member = done[0][0]
        for p in range(2):
            row = 2 * i + p
            for side in range(2):
                part = slice(side * SPAN, (side + 1) * SPAN)
                value = done[side][1][p] + e_ref[member, row + 2, part, :].astype(F32)
                for lane in range(3):
                    b_ref[2 * n + p, lane, pl.ds(side, SPAN, stride=2), :] = value[
                        :, lane * 128 : (lane + 1) * 128
                    ]
            for lane in range(3):
                out_ref[member, row, :, lane * 128 : (lane + 1) * 128] = b_ref[
                    2 * n + p, lane
                ].astype(BF)

    def products(step, k):
        x_ref, m_ref = x_refs[step % 2], m_refs[step % 2]
        count = (I1 if step < 8 else I2) * SPAN
        x = [x_ref[k, j, :count, :] for j in range(4)]
        even, odd, both = [jnp.concatenate(part, axis=1) for part in (x[:3], x[1:], x)]
        if step < 8:
            halo = hx_refs[step % 2][k].astype(BF)
            even = jnp.concatenate([even, halo], axis=0)
            none = jnp.zeros((HALO_ROWS, C), BF)
            both = jnp.concatenate([both, jnp.concatenate([halo, none], axis=1)], axis=0)
        slot = step % 2
        none = jnp.zeros((C, 128), BF)
        shared = jnp.concatenate(
            [
                jnp.concatenate([w_ref[slot, k, :, 256:], none], axis=0),
                jnp.concatenate([none, w_ref[slot, k, :, :128]], axis=0),
            ],
            axis=1,
        )
        low = jnp.dot(even, w_ref[slot, k, :, :256], preferred_element_type=F32)
        middle = jnp.dot(both, shared, preferred_element_type=F32)
        high = jnp.dot(odd, w_ref[slot, k, :, 128:], preferred_element_type=F32)
        m_ref[k, :count, :256] = low[:count]
        m_ref[k, :count, 256:] = middle[:count, :128]
        m_ref[k, count : 2 * count, :128] = middle[:count, 128:]
        m_ref[k, count : 2 * count, 128:] = high
        if step < 8:
            m_ref[k, 2 * count : 2 * count + HALO_ROWS, :256] = low[count:]
            m_ref[k, 2 * count : 2 * count + HALO_ROWS, 256:] = middle[count:, :128]

    def run(step):
        arrive(step)
        if step < 11:
            fetch(step + 1)
        builds = step < 11
        settles = step > 0
        pieces = step < PIECES // QUARTERS
        if settles and step < 9:
            settle_halo(step - 1)
            settle_first(step - 1, I1 - 1)

        @pl.loop(0, QUARTERS)
        def _(k):
            if pieces:
                piece_in(step, k)
            products(step, k)
            for n in range(QUARTER if settles else 0):
                if step < 9:
                    settle_first(step - 1, QUARTER * k + n)
                else:
                    settle_second(step - 1, QUARTER * k + n, n)
            if step == 7:
                for n in range(QUARTER):
                    build(8, jnp.maximum(QUARTER * k + n - 1, 0))
            elif step < 7:
                build(step + 1, QUARTER * k, QUARTER + 1)
                build_halo(step + 1, k)
            elif builds:
                build(step + 1, QUARTER * k, QUARTER)
            if pieces:
                piece_made(step, k)
                piece_out(step, k)

        if step == PIECES // QUARTERS - 1:
            for k in range(QUARTERS):
                made_copy(QUARTERS * step + k, k).wait()
        if step == 7:
            build(8, I2 - 1)

    @pl.loop(0, I1 // 4)
    def _(block):
        build(0, 4 * block, 5)

    for quarter in range(QUARTERS):
        build_halo(0, quarter)

    for step in range(12):
        run(step)

    first_out = pltpu.make_async_copy(out_ref.at[0], out_hbm.at[0], out_sem.at[QUARTERS])
    first_out.start()

    def second_out(k):
        rows = pl.ds(2 * QUARTER * k, 2 * QUARTER)
        return pltpu.make_async_copy(out_ref.at[1, rows], out_hbm.at[1, rows], out_sem.at[k])

    @pl.loop(0, QUARTERS)
    def _(k):
        for n in range(QUARTER):
            settle_second(11, QUARTER * k + n, n)
        second_out(k).start()

    first_out.wait()
    for k in range(QUARTERS):
        second_out(k).wait()


def block_call(*operands):
    vmem = pl.BlockSpec(memory_space=pltpu.VMEM)
    smem = pl.BlockSpec(memory_space=pltpu.SMEM)
    hbm = pl.BlockSpec(memory_space=pl.ANY)
    m1 = 2 * I1 * SPAN + HALO_ROWS
    return pl.pallas_call(
        main_kernel,
        in_specs=[smem, vmem, vmem, vmem, vmem, hbm, hbm, hbm],
        out_specs=[hbm, hbm],
        out_shape=[
            jax.ShapeDtypeStruct((2, ROWS, COLS, C), BF),
            jax.ShapeDtypeStruct((SETS, K3, C), BF),
        ],
        scratch_shapes=[
            pltpu.VMEM((9, 38 * 16, CELLS), BF),
            pltpu.VMEM((6, R1, 4, SPAN, C), BF),
            pltpu.VMEM((6, 2, HALO_ROWS, K3), F32),
            pltpu.VMEM((R2, 4, SPAN, C), BF),
            pltpu.VMEM((R2, 4, SPAN, C), BF),
            pltpu.VMEM((R2, 4, SPAN, C), BF),
            pltpu.VMEM((R2, 4, SPAN, C), BF),
            pltpu.VMEM((2, R1, COLS, C), BF),
            pltpu.VMEM((4, 4, I1 * SPAN, C), BF),
            pltpu.VMEM((4, 4, I1 * SPAN, C), BF),
            pltpu.VMEM((4, HALO_ROWS, K3), F32),
            pltpu.VMEM((4, HALO_ROWS, K3), F32),
            pltpu.VMEM((4, m1, C), F32),
            pltpu.VMEM((4, m1, C), F32),
            pltpu.VMEM((2, 2, m1, C), F32),
            pltpu.VMEM((2, 4, K3, C), BF),
            pltpu.VMEM((ENTRY_ROWS, USED, C), F32),
            pltpu.VMEM((2 * QUARTER, 3, COLS, 128), F32),
            pltpu.VMEM((2, HALO_ROWS, C), F32),
            pltpu.VMEM((USED, 128), F32),
            pltpu.VMEM((QUARTERS, 3, 3, PIECE, C), BF),
            pltpu.VMEM((QUARTERS, SETS, PIECE, C), BF),
            pltpu.VMEM((2, ROWS, COLS, C), BF),
            pltpu.SemaphoreType.DMA((2, 3)),
            pltpu.SemaphoreType.DMA((QUARTERS,)),
            pltpu.SemaphoreType.DMA((QUARTERS,)),
            pltpu.SemaphoreType.DMA((QUARTERS + 1,)),
        ],
        compiler_params=pltpu.CompilerParams(vmem_limit_bytes=62 * MIB),
        name="block",
    )(*operands)[0]


def body(latent, clip_lengths, entry_kernel, first_gain, first_kernel, second_gain, second_kernel):
    everything, u1 = gathered(latent.transpose(0, 1, 3, 2), first_kernel)
    return block_call(
        clip_lengths,
        everything,
        entry_kernel.reshape(27 * 16, C),
        first_gain,
        second_gain,
        first_kernel.reshape(3, 3, K3, C),
        second_kernel.reshape(3, 3, K3, C),
        u1.reshape(SETS, K3, C),
    )


def solution(mesh):
    return jax.shard_map(
        body,
        mesh=mesh,
        in_specs=(P("tm", "sy", "sx", None), P(), P(), P(), P(), P(), P()),
        out_specs=P("tm", "sy", "sx", None),
        check_vma=False,
    )
```
